32 devices in a mesh: section: 2 (over core), dp: 16 (over z, y, x).
Axes of the slice: x: 2, y: 2, z: 4, core: 2. Of those that a mesh axis runs over, the one named last changes fastest.
Arguments:
- tokens: bfloat16 [16384, 768], P('dp'), may hold values from -6 to 6
- heights: int32 [64], P('dp'), may hold values from 1 to 15, as said below
- out_grad: bfloat16 [16384, 768], P('dp'), may hold values from -6 to 6
- w_query: bfloat16 [2, 768, 768], P('section', 'dp'), may hold values from -0.21875 to 0.21875
- w_key: bfloat16 [2, 768, 768], P('section', 'dp'), may hold values from -0.21875 to 0.21875
- w_value: bfloat16 [2, 768, 768], P('section', 'dp'), may hold values from -0.21875 to 0.21875
- w_out: bfloat16 [2, 768, 768], P('section', 'dp'), may hold values from -0.875 to 0.875
- w_gate: bfloat16 [2, 768, 2048], P('section', 'dp'), may hold values from -0.21875 to 0.21875
- w_up: bfloat16 [2, 768, 2048], P('section', 'dp'), may hold values from -0.21875 to 0.21875
- w_down: bfloat16 [2, 2048, 768], P('section', 'dp'), may hold values from -0.125 to 0.125
- gain_attn: bfloat16 [2, 768], P('section', 'dp'), may hold values from 0.5 to 1.5
- gain_ffn: bfloat16 [2, 768], P('section', 'dp'), may hold values from 0.5 to 1.5
Outputs:
- activations: bfloat16 [2, 16384, 768], P('section', 'dp')
- input_grads: bfloat16 [2, 16384, 768], P('section', 'dp')
- grad_query: float32 [2, 768, 768], P('section', 'dp')
- grad_key: float32 [2, 768, 768], P('section', 'dp')
- grad_value: float32 [2, 768, 768], P('section', 'dp')
- grad_out: float32 [2, 768, 768], P('section', 'dp')
- grad_gate: float32 [2, 768, 2048], P('section', 'dp')
- grad_up: float32 [2, 768, 2048], P('section', 'dp')
- grad_down: float32 [2, 2048, 768], P('section', 'dp')
- grad_gain_attn: float32 [2, 768], P('section', 'dp')
- grad_gain_ffn: float32 [2, 768], P('section', 'dp')
The draws below stay inside these ranges and needn't reach their ends.
Inputs may be any that keep to these rules, and one draw needn't show every extreme that they name: `heights`: rows of each cropped image; in every draw some image has 15 rows and some has 1.
All inputs are finite; a program needn't handle non-finite values.
Results may differ from the reference program's by a relative error of at most 0.02.
Values may be sent and summed in bfloat16 or wider, within the bound.
No kernel may reach another device: no remote copies, remote signals or barrier semaphores. Data moves between devices by JAX's collectives and lax.ppermute only.
A program may use at most 256 MiB of HBM per device.

```python
import jax
import jax.numpy as jnp
from jax import lax

D = 768
HEADS = 12
HEAD_DIM = 64
FF = 2048
WIDE = 16
HMAX = 15
SLOT = 256
IMAGES = 64
TOKENS = 16384
N_DP = 16


def draw_heights(key, part):
    key = jax.random.fold_in(key, 11)
    key_rows, key_top, key_low = jax.random.split(key, 3)
    rows_drawn = jax.random.randint(key_rows, (IMAGES,), 1, HMAX + 1)
    top_index = jax.random.randint(key_top, (), 0, IMAGES)
    step_off = jax.random.randint(key_low, (), 1, IMAGES)
    low_index = (top_index + step_off) % IMAGES
    rows_drawn = rows_drawn.at[top_index].set(HMAX)
    rows_drawn = rows_drawn.at[low_index].set(1)
    return rows_drawn.astype(jnp.int32)


def spiked(values, own_key, source, target, blocks, factor):
    def block_of(axis_at):
        return (jnp.arange(values.shape[axis_at]) // (values.shape[axis_at] // blocks)).reshape((-1,) + (1,) * (values.ndim - 1 - axis_at))

    one_side = jax.random.permutation(own_key, blocks)[block_of(target)]
    far = (block_of(target) + blocks // 2) % blocks
    return jnp.where((block_of(source) == one_side) | (block_of(source) == far), factor * values, values)


def steps_of(rng, shape, cuts, least, largest):
    gain = 1.0
    for dim, parts in cuts:
        steps = jax.random.uniform(jax.random.fold_in(jax.random.fold_in(rng, 6), dim), (parts,), jnp.float32, least / len(cuts), largest / len(cuts))
        gain = gain * jnp.repeat(jnp.exp(steps), shape[dim] // parts).reshape((-1,) + (1,) * (len(shape) - 1 - dim))
    return gain


def centred(own_key, extent, width, reach, shards=(), held_as=jnp.bfloat16):
    result = jax.random.normal(own_key, extent, jnp.float32) * width
    if len(shards) > 0:
        result = steps_of(own_key, extent, shards, -0.22, 0.18) * result
    return jnp.clip(result, min=-reach, max=reach).astype(held_as)


def heavy_noise(stream_key, dims, scale, reach, cuts, heavy, dtype=jnp.bfloat16):
    values = scale * jax.random.normal(stream_key, dims, jnp.float32)
    if cuts:
        values = values * steps_of(stream_key, dims, cuts, -0.22, 0.18)
    return jnp.clip(spiked(values, jax.random.fold_in(stream_key, 3), *heavy), -reach, reach).astype(dtype)


def setup_inputs(seed: int = 0) -> dict:
    key_list = jax.random.split(jax.random.key(seed), 13)
    return {
        "tokens": heavy_noise(key_list[0], (TOKENS, D), 1.0, 6.0, ((0, 16),), (0, 1, 16, 2.0)),
        "heights": draw_heights(jax.random.fold_in(key_list[12], 71), 0),
        "out_grad": centred(key_list[2], (TOKENS, D), 1.0, 6.0, ((0, 16),)),
        "w_query": centred(key_list[3], (2, D, D), D ** -0.5, 0.21875, ((0, 2), (1, 16))),
        "w_key": centred(key_list[4], (2, D, D), D ** -0.5, 0.21875, ((0, 2), (1, 16))),
        "w_value": centred(key_list[5], (2, D, D), D ** -0.5, 0.21875, ((0, 2), (1, 16))),
        "w_out": centred(key_list[6], (2, D, D), (D // 16) ** -0.5, 0.875, ((0, 2), (1, 16))),
        "w_gate": centred(key_list[7], (2, D, FF), D ** -0.5, 0.21875, ((0, 2), (1, 16))),
        "w_up": centred(key_list[8], (2, D, FF), D ** -0.5, 0.21875, ((0, 2), (1, 16))),
        "w_down": centred(key_list[9], (2, FF, D), FF ** -0.5, 0.125, ((0, 2), (1, 16))),
        "gain_attn": jnp.clip(1.0 + 0.1 * jax.random.normal(key_list[10], (2, D), jnp.float32), 0.5, 1.5).astype(jnp.bfloat16),
        "gain_ffn": jnp.clip(1.0 + 0.1 * jax.random.normal(key_list[11], (2, D), jnp.float32), 0.5, 1.5).astype(jnp.bfloat16),
    }


@jax.custom_vjp
def low(v):
    return lax.optimization_barrier(v.astype(jnp.bfloat16)).astype(jnp.float32)

@jax.custom_vjp
def low_back(v):
    return v

def low_keep(v):
    return (low(v), None)

def low_pass(kept, grad):
    return (grad,)

def back_keep(v):
    return (v, None)

def back_low(kept, grad):
    return (low(grad),)
low.defvjp(low_keep, low_pass)
low_back.defvjp(back_keep, back_low)
EPS = 1e-05
SCALE = 0.125

def rope_tables(slot_len):
    position = jnp.arange(slot_len)
    index = jnp.maximum(position - 1, 0)
    started = (position > 0).astype(jnp.float32)
    row_pos = (index // WIDE).astype(jnp.float32) * started
    col_pos = (index % WIDE).astype(jnp.float32) * started
    quarter = HEAD_DIM // 4
    freq = 10000.0 ** (-jnp.arange(quarter).astype(jnp.float32) / quarter)
    row_angle = row_pos[:, None] * freq[None, :]
    col_angle = col_pos[:, None] * freq[None, :]
    angle = jnp.stack([row_angle, row_angle, col_angle, col_angle], axis=1).reshape(slot_len, 1, HEAD_DIM)
    angle = jnp.tile(angle, (1, HEADS, 1)).reshape(slot_len, HEADS * HEAD_DIM)
    return (jnp.cos(angle), jnp.sin(angle))

def rotate(values):
    leading = values.shape[:-1]
    pieces = values.reshape(leading + (values.shape[-1] // HEAD_DIM, 4, HEAD_DIM // 4))
    turned = jnp.stack([-pieces[..., 1, :], pieces[..., 0, :], -pieces[..., 3, :], pieces[..., 2, :]], axis=-2)
    return turned.reshape(values.shape)

def apply_rope(values, cosine, sine_table):
    return values * cosine + rotate(values) * sine_table

def rms_scale(values):
    return lax.rsqrt(lax.optimization_barrier(jnp.mean(values * values, axis=-1, keepdims=True)) + EPS)

def project(left, weight):
    return jnp.einsum('bsd,de->bse', left, weight, precision=lax.Precision.HIGHEST)

def block(inputs, lengths, params):
    w_q, w_k, w_v, w_o, w_g, w_u, w_d, gain_one, gain_two = params
    batch_size, slot_len, model_width = inputs.shape
    cosine, sine_table = rope_tables(slot_len)
    position = jnp.arange(slot_len)
    limit_len = WIDE * lengths + 1
    valid_rows = (position[None, :] < limit_len[:, None]).astype(jnp.float32)[:, :, None]
    causal = position[None, :] <= position[:, None]
    attn_mask = causal[None, None, :, :] & (position[None, :] < limit_len[:, None])[:, None, None, :]
    inputs = low_back(inputs)
    normed = low(inputs * rms_scale(inputs) * gain_one)
    query_rot = low(apply_rope(low_back(project(normed, w_q)), cosine, sine_table))
    key_rot = low(apply_rope(low_back(project(normed, w_k)), cosine, sine_table))
    value_low = low(low_back(project(normed, w_v)))
    shape_four = (batch_size, slot_len, HEADS, HEAD_DIM)
    scores = jnp.einsum('bqhd,bkhd->bhqk', query_rot.reshape(shape_four), key_rot.reshape(shape_four), precision=lax.Precision.HIGHEST) * SCALE
    scores = low_back(scores)
    scores = jnp.where(attn_mask, scores, -1e+30)
    probs_full = jax.nn.softmax(scores, axis=-1)
    probs_low = low(probs_full)
    mixed = jnp.einsum('bhqk,bkhd->bqhd', probs_low, value_low.reshape(shape_four), precision=lax.Precision.HIGHEST).reshape(batch_size, slot_len, model_width)
    mixed_low = low(low_back(mixed))
    branch_out = low_back(project(mixed_low, w_o))
    middle = inputs + branch_out
    normed_two = low(middle * rms_scale(middle) * gain_two)
    gate_raw = low_back(project(normed_two, w_g))
    up_raw = low_back(project(normed_two, w_u))
    hidden_low = low(jax.nn.silu(gate_raw) * up_raw)
    ffn_out = low_back(project(hidden_low, w_d))
    return valid_rows * (middle + ffn_out)

def layer_all(inputs, heights, params):
    groups = inputs.reshape(N_DP, -1, SLOT, D)
    group_lengths = heights.reshape(N_DP, -1)

    def run_group(group_pair):
        return block(group_pair[0], group_pair[1], params)
    outputs = lax.map(jax.checkpoint(run_group), (groups, group_lengths))
    return outputs.reshape(IMAGES, SLOT, D)

def reference(tokens, heights, out_grad, w_query, w_key, w_value, w_out, w_gate, w_up, w_down, gain_attn, gain_ffn):
    stacked = (w_query, w_key, w_value, w_out, w_gate, w_up, w_down, gain_attn, gain_ffn)
    first_params = tuple((weight[0].astype(jnp.float32) for weight in stacked))
    second_params = tuple((weight[1].astype(jnp.float32) for weight in stacked))
    start_act = tokens.astype(jnp.float32).reshape(IMAGES, SLOT, D)

    def apply_layer(inputs, params):
        return layer_all(inputs, heights, params)
    first_out, back_first = jax.vjp(apply_layer, start_act, first_params)
    second_in = first_out.astype(jnp.bfloat16).astype(jnp.float32)
    second_out, back_second = jax.vjp(apply_layer, second_in, second_params)
    grad_mid, grads_second = back_second(out_grad.astype(jnp.float32).reshape(IMAGES, SLOT, D))
    grad_start, grads_first = back_first(grad_mid)
    activations = jnp.stack([first_out, second_out]).astype(jnp.bfloat16).reshape(2, TOKENS, D)
    input_grads = jnp.stack([grad_start, grad_mid]).astype(jnp.bfloat16).reshape(2, TOKENS, D)
    paired = [jnp.stack([one_grad, two_grad]) for one_grad, two_grad in zip(grads_first, grads_second)]
    return (activations, input_grads, paired[0], paired[1], paired[2], paired[3], paired[4], paired[5], paired[6], paired[7], paired[8])
```

```python
import functools

import jax
import jax.numpy as jnp
import numpy as np
from jax import lax
from jax.experimental import pallas as pl
from jax.experimental.pallas import tpu as pltpu
from jax.sharding import PartitionSpec as P

D = 768
HEADS = 12
HEAD_DIM = 64
FF = 2048
WIDE = 16
SLOT = 256
HALF = D // 2
FHALF = FF // 2
PAIRS = HEADS // 2
LANES = 128
EPS = 1e-05
SCALE = 0.125
F32 = jnp.float32
BF16 = jnp.bfloat16
VMEM_BYTES = 56 * 1024 * 1024

X, Y, ZL, ZH = 1, 2, 4, 8
GATHER_ORDERS = (
    (ZH, Y, X, ZL),
    (ZH, ZL, X, Y),
    (ZH, Y, ZL, X),
    (ZL, X, ZH, Y),
    (ZH, Y, X, ZL),
    (ZH, ZL, Y, X),
)
SCATTER_ORDERS = ((X, Y, ZL, ZH), (Y, X, ZL, ZH))


def order_masks(order):
    masks = [0]
    for bit in order:
        masks = masks + [m ^ bit for m in masks]
    return masks


def flip(value, bit, count):
    return lax.ppermute(value, "dp", [(i, i ^ bit) for i in range(count)])


def swap(value):
    return lax.ppermute(value, "section", [(0, 1), (1, 0)])


def rope_consts():
    position = np.arange(SLOT)
    index = np.maximum(position - 1, 0)
    started = (position > 0).astype(np.float32)
    row_pos = (index // WIDE).astype(np.float32) * started
    col_pos = (index % WIDE).astype(np.float32) * started
    quarter = HEAD_DIM // 4
    freq = np.power(np.float32(10000.0), -np.arange(quarter, dtype=np.float32) / quarter)
    row_angle = row_pos[:, None] * freq[None, :]
    col_angle = col_pos[:, None] * freq[None, :]
    angle = np.concatenate([row_angle, row_angle, col_angle, col_angle], axis=1)
    angle = np.concatenate([angle, angle], axis=1).astype(np.float32)
    even = (np.arange(LANES) // quarter) % 2 == 0
    sine = np.sin(angle)
    return (
        np.cos(angle).astype(np.float32),
        np.where(even, -sine, 0.0).astype(np.float32),
        np.where(even, 0.0, sine).astype(np.float32),
    )


def dot(left, right):
    return jnp.dot(left, right, preferred_element_type=F32)


def dot_nt(left, right):
    return lax.dot_general(left, right, (((1,), (1,)), ((), ())), preferred_element_type=F32)


def dot_tn(left, right):
    return lax.dot_general(left, right, (((0,), (0,)), ((), ())), preferred_element_type=F32)


def turn(value, sin_a, sin_b):
    return pltpu.roll(value, LANES - 16, 1) * sin_a + pltpu.roll(value, 16, 1) * sin_b


def params(steps=1):
    return pltpu.CompilerParams(
        dimension_semantics=("arbitrary",) * steps, vmem_limit_bytes=VMEM_BYTES
    )


def cost(flops, nbytes):
    return pl.CostEstimate(flops=int(flops), bytes_accessed=int(nbytes), transcendentals=0)


def shape(*dims, dtype=BF16):
    return jax.ShapeDtypeStruct(dims, dtype)


def launch(kernel, prefetch, grid, inputs, in_specs, out_shape, out_specs, work, scratch=(), after=()):
    first = len(prefetch) + len(inputs)
    extra = len(after)

    def body(*refs):
        kernel(*refs[:first], *refs[first + extra :])

    return pl.pallas_call(
        body,
        grid_spec=pltpu.PrefetchScalarGridSpec(
            num_scalar_prefetch=len(prefetch),
            grid=grid,
            in_specs=list(in_specs) + [pl.BlockSpec(memory_space=pl.ANY)] * extra,
            out_specs=out_specs,
            scratch_shapes=list(scratch),
        ),
        out_shape=out_shape,
        compiler_params=params(len(grid)),
        cost_estimate=work,
    )(*prefetch, *inputs, *after)


def head_split(pair):
    lane = lax.broadcasted_iota(jnp.int32, pair.shape, 1)
    zero = jnp.zeros_like(pair)
    return jnp.where(lane < HEAD_DIM, pair, zero), jnp.where(lane < HEAD_DIM, zero, pair)


def attention_kernel(
    info, lim, x_ref, wq, wk, wv, cos, sin_a, sin_b, act_ref, qkv_ref, probs_ref, scale_ref
):
    image = pl.program_id(0)
    x = x_ref[...].astype(F32)
    r = lax.rsqrt(jnp.mean(x * x, axis=1, keepdims=True) + EPS)
    normed = (x * r).astype(BF16)
    act_ref[:, :D] = normed
    scale_ref[...] = jnp.broadcast_to(r, (SLOT, LANES))
    for part, weight in enumerate((wq, wk)):
        full = dot(normed, weight[...])
        for p in range(PAIRS):
            piece = full[:, p * LANES : (p + 1) * LANES]
            piece = piece * cos[...] + turn(piece, sin_a[...], sin_b[...])
            start = part * D + p * LANES
            qkv_ref[:, start : start + LANES] = piece.astype(BF16)
    qkv_ref[:, 2 * D :] = dot(normed, wv[...]).astype(BF16)
    row = lax.broadcasted_iota(jnp.int32, (SLOT, SLOT), 0)
    col = lax.broadcasted_iota(jnp.int32, (SLOT, SLOT), 1)
    mask = (col <= row) & (col < lim[info[1] * 2 + image])
    for p in range(PAIRS):
        lanes = slice(p * LANES, (p + 1) * LANES)
        query = qkv_ref[:, lanes]
        keys = head_split(qkv_ref[:, D + p * LANES : D + (p + 1) * LANES])
        values = head_split(qkv_ref[:, 2 * D + p * LANES : 2 * D + (p + 1) * LANES])
        probs = []
        for h in range(2):
            scores = jnp.where(mask, dot_nt(query, keys[h]), -1e30)
            top = jnp.max(scores, axis=1, keepdims=True)
            raised = jnp.exp(scores - top)
            total = jnp.sum(raised, axis=1, keepdims=True)
            probs.append((raised * (1.0 / total)).astype(BF16))
            probs_ref[0, 2 * p + h] = probs[h]
        mixed = dot(jnp.concatenate(probs, axis=1), jnp.concatenate(values, axis=0))
        act_ref[:, D + p * LANES : D + (p + 1) * LANES] = mixed.astype(BF16)


def attention(info, lim, x, x_rows, wq, wk, wv, tables, after=()):
    whole = lambda i, info, lim: (0, 0)
    table = pl.BlockSpec((SLOT, LANES), whole)
    weight = pl.BlockSpec((D, D), whole)
    return launch(
        attention_kernel,
        (info, lim,),
        (2,),
        (x, wq, wk, wv, *tables,),
        [
                pl.BlockSpec((SLOT, D), lambda i, info, lim: (info[x_rows] * 2 + i, 0)),
                weight,
                weight,
                weight,
                table,
                table,
                table,
            ],
        [
            shape(2 * SLOT, 2 * D),
            shape(2 * SLOT, 3 * D),
            shape(2, HEADS, SLOT, SLOT),
            shape(2 * SLOT, LANES, dtype=F32),
        ],
        [
                pl.BlockSpec((SLOT, 2 * D), lambda i, info, lim: (i, 0)),
                pl.BlockSpec((SLOT, 3 * D), lambda i, info, lim: (i, 0)),
                pl.BlockSpec((1, HEADS, SLOT, SLOT), lambda i, info, lim: (i, 0, 0, 0)),
                pl.BlockSpec((SLOT, LANES), lambda i, info, lim: (i, 0)),
            ],
        cost(3.6e9 + 24 * 4 * 256 * 256 * 128, 12e6),
        (),
        after,
    )


FBLOCK = 512


def feed_kernel(
    info, x_ref, mixed_ref, wo, wg, wu, middle_ref, normed_ref, scale_ref, hid_ref, s1_ref, s2_ref
):
    step = pl.program_id(0)

    @pl.when(step == 0)
    def _():
        middle = x_ref[...].astype(F32) + dot(mixed_ref[...], wo[...])
        r = lax.rsqrt(jnp.mean(middle * middle, axis=1, keepdims=True) + EPS)
        middle_ref[...] = middle
        normed_ref[...] = (middle * r).astype(BF16)
        scale_ref[...] = jnp.broadcast_to(r, scale_ref.shape)

    gate = dot(normed_ref[...], wg[...])
    up = dot(normed_ref[...], wu[...])
    sig = 1.0 / (1.0 + jnp.exp(-gate))
    silu = gate * sig
    hid_ref[...] = (silu * up).astype(BF16)
    s1_ref[...] = (up * (sig * (1.0 + gate * (1.0 - sig)))).astype(BF16)
    s2_ref[...] = silu.astype(BF16)


def feed(info, x, x_rows, act, wo, wg, wu, after=()):
    rows = 2 * SLOT
    whole = lambda j, info: (0, 0)
    col = pl.BlockSpec((D, FBLOCK), lambda j, info: (0, j))
    wide = pl.BlockSpec((rows, FBLOCK), lambda j, info: (0, j))
    return launch(
        feed_kernel,
        (info,),
        (FF // FBLOCK,),
        (x, act, wo, wg, wu,),
        [
                pl.BlockSpec((rows, D), lambda j, info: (info[x_rows], 0)),
                pl.BlockSpec((rows, D), lambda j, info: (0, 1)),
                pl.BlockSpec((D, D), whole),
                col,
                col,
            ],
        [
            shape(rows, D, dtype=F32),
            shape(rows, D),
            shape(rows, LANES, dtype=F32),
            shape(rows, FF),
            shape(rows, FF),
            shape(rows, FF),
        ],
        [
                pl.BlockSpec((rows, D), whole),
                pl.BlockSpec((rows, D), whole),
                pl.BlockSpec((rows, LANES), whole),
                wide,
                wide,
                wide,
            ],
        cost(2 * rows * D * (D + 2 * FF), 18e6),
        (),
        after,
    )


def leave_kernel(info, lim, middle_ref, hid_ref, wd, out_ref):
    image = pl.program_id(0)
    result = middle_ref[...] + dot(hid_ref[...], wd[...])
    row = lax.broadcasted_iota(jnp.int32, result.shape, 0)
    out_ref[...] = jnp.where(row < lim[info[1] * 2 + image], result, 0.0).astype(BF16)


def leave(info, lim, middle, hidden, wd, after=()):
    rows = 2 * SLOT
    return launch(
        leave_kernel,
        (info, lim,),
        (2,),
        (middle, hidden, wd,),
        [
                pl.BlockSpec((SLOT, D), lambda i, info, lim: (i, 0)),
                pl.BlockSpec((SLOT, FF), lambda i, info, lim: (i, 0)),
                pl.BlockSpec((FF, D), lambda i, info, lim: (0, 0)),
            ],
        shape(rows, D),
        pl.BlockSpec((SLOT, D), lambda i, info, lim: (i, 0)),
        cost(2 * rows * D * FF, 8e6),
        (),
        after,
    )


def feed_back_kernel(
    info,
    grad_ref,
    wd,
    wg,
    wu,
    s1_ref,
    s2_ref,
    normed_ref,
    scale_ref,
    wo,
    keep_ref,
    send_ref,
    gmid_ref,
    gz_ref,
    gmix_ref,
    total,
):
    step = pl.program_id(0)
    per_half = FHALF // FBLOCK
    grad_hidden = dot_nt(grad_ref[...], wd[...])
    ggate = (grad_hidden * s1_ref[...].astype(F32)).astype(BF16)
    gup = (grad_hidden * s2_ref[...].astype(F32)).astype(BF16)
    at = pl.multiple_of((step % per_half) * FBLOCK, FBLOCK)
    own = (step // per_half) == info[1]

    @pl.when(own)
    def _():
        keep_ref[:, pl.ds(at, FBLOCK)] = ggate
        keep_ref[:, pl.ds(at + FHALF, FBLOCK)] = gup

    @pl.when(jnp.logical_not(own))
    def _():
        send_ref[:, pl.ds(at, FBLOCK)] = ggate
        send_ref[:, pl.ds(at + FHALF, FBLOCK)] = gup

    part = dot_nt(ggate, wg[...]) + dot_nt(gup, wu[...])

    @pl.when(step == 0)
    def _():
        total[...] = part

    @pl.when(step > 0)
    def _():
        total[...] += part

    @pl.when(step == pl.num_programs(0) - 1)
    def _():
        gn = total[...]
        normed = normed_ref[...].astype(F32)
        mean = jnp.mean(gn * normed, axis=1, keepdims=True)
        gmid = grad_ref[...].astype(F32) + scale_ref[:, :1] * (gn - normed * mean)
        gz = gmid.astype(BF16)
        gmid_ref[...] = gmid
        gz_ref[...] = gz
        gmix_ref[...] = dot_nt(gz, wo[...]).astype(BF16)


def feed_back(info, grad, grad_rows, wd, wg, wu, s1, s2, normed, scale, wo, after=()):
    rows = 2 * SLOT
    whole = lambda j, info: (0, 0)
    col = pl.BlockSpec((D, FBLOCK), lambda j, info: (0, j))
    wide = pl.BlockSpec((rows, FBLOCK), lambda j, info: (0, j))
    full = pl.BlockSpec((rows, D), whole)
    return launch(
        feed_back_kernel,
        (info,),
        (FF // FBLOCK,),
        (grad, wd, wg, wu, s1, s2, normed, scale, wo,),
        [
                pl.BlockSpec((rows, D), lambda j, info: (info[grad_rows], 0)),
                pl.BlockSpec((FBLOCK, D), lambda j, info: (j, 0)),
                col,
                col,
                wide,
                wide,
                full,
                pl.BlockSpec((rows, LANES), whole),
                pl.BlockSpec((D, D), whole),
            ],
        [
            shape(rows, FF),
            shape(rows, FF),
            shape(rows, D, dtype=F32),
            shape(rows, D),
            shape(rows, D),
        ],
        [
                pl.BlockSpec((rows, FF), whole),
                pl.BlockSpec((rows, FF), whole),
                full,
                full,
                full,
            ],
        cost(2 * rows * D * (3 * FF + D), 24e6),
        [pltpu.VMEM((rows, D), F32)],
        after,
    )


def attention_back_kernel(
    info,
    gmix_ref,
    qkv_ref,
    probs_ref,
    wq,
    wk,
    wv,
    normed_ref,
    scale_ref,
    gmid_ref,
    gz_ref,
    cos,
    sin_a,
    sin_b,
    gin_ref,
    keep_ref,
    send_ref,
    grads,
):
    for p in range(PAIRS):
        lanes = slice(p * LANES, (p + 1) * LANES)
        gmix = gmix_ref[:, lanes]
        query = head_split(qkv_ref[:, lanes])
        keys = head_split(qkv_ref[:, D + p * LANES : D + (p + 1) * LANES])
        values = head_split(qkv_ref[:, 2 * D + p * LANES : 2 * D + (p + 1) * LANES])
        gmix_parts = head_split(gmix)
        gs_parts = []
        for h in range(2):
            probs = probs_ref[0, 2 * p + h].astype(F32)
            weighted = probs * dot_nt(gmix, values[h])
            inner = jnp.sum(weighted, axis=1, keepdims=True)
            gs_parts.append((weighted - probs * inner).astype(BF16))
        gq = dot(jnp.concatenate(gs_parts, axis=1), jnp.concatenate(keys, axis=0))
        gk = dot_tn(gs_parts[0], query[0]) + dot_tn(gs_parts[1], query[1])
        gv = dot_tn(probs_ref[0, 2 * p], gmix_parts[0]) + dot_tn(
            probs_ref[0, 2 * p + 1], gmix_parts[1]
        )
        gq = gq * cos[...] - turn(gq, sin_a[...], sin_b[...])
        gk = gk * cos[...] - turn(gk, sin_a[...], sin_b[...])
        grads[0, :, lanes] = gq.astype(BF16)
        grads[1, :, lanes] = gk.astype(BF16)
        grads[2, :, lanes] = gv.astype(BF16)
    gn = dot_nt(grads[0], wq[...]) + dot_nt(grads[1], wk[...]) + dot_nt(grads[2], wv[...])
    normed = normed_ref[...].astype(F32)
    mean = jnp.mean(gn * normed, axis=1, keepdims=True)
    gin = gmid_ref[...] + scale_ref[:, :1] * (gn - normed * mean)
    gin_ref[...] = gin.astype(BF16)
    for h in range(2):

        @pl.when(info[1] == h)
        def _():
            for out, half in ((keep_ref, h), (send_ref, 1 - h)):
                cols = slice(half * HALF, (half + 1) * HALF)
                out[:, :HALF] = gz_ref[:, cols]
                for part in range(3):
                    out[:, (part + 1) * HALF : (part + 2) * HALF] = grads[part, :, cols]


def attention_back(info, gmix, qkv, probs, wq, wk, wv, act, scale, gmid, gz, tables, after=()):
    rows = 2 * SLOT
    whole = lambda i, info: (0, 0)
    table = pl.BlockSpec((SLOT, LANES), whole)
    weight = pl.BlockSpec((D, D), whole)
    full = pl.BlockSpec((SLOT, D), lambda i, info: (i, 0))
    pack = pl.BlockSpec((SLOT, 4 * HALF), lambda i, info: (i, 0))
    return launch(
        attention_back_kernel,
        (info,),
        (2,),
        (gmix, qkv, probs, wq, wk, wv, act, scale, gmid, gz, *tables,),
        [
                full,
                pl.BlockSpec((SLOT, 3 * D), lambda i, info: (i, 0)),
                pl.BlockSpec((1, HEADS, SLOT, SLOT), lambda i, info: (i, 0, 0, 0)),
                weight,
                weight,
                weight,
                full,
                pl.BlockSpec((SLOT, LANES), lambda i, info: (i, 0)),
                full,
                full,
                table,
                table,
                table,
            ],
        [shape(rows, D), shape(rows, 4 * HALF), shape(rows, 4 * HALF)],
        [full, pack, pack],
        cost(2 * rows * D * 3 * D + 24 * 8 * 256 * 256 * 128, 16e6),
        [pltpu.VMEM((3, SLOT, D), BF16)],
        after,
    )


def spread(info, scratch, rows, row_from, row_count, lane_blocks, masks, keep, send, row_to):
    for place, mask in enumerate(masks):
        shard = info[0] ^ mask
        at = pl.multiple_of(shard * rows + row_from, 16)
        out = keep if place < 8 else send
        for block in range(lane_blocks):
            out[place % 8, pl.ds(row_to + block * row_count, row_count), :] = scratch[
                pl.ds(at, row_count), block * LANES : (block + 1) * LANES
            ]


def feed_weight_kernel(
    masks_p,
    masks_q,
    info,
    own_ref,
    oth_ref,
    g_own,
    g_oth,
    hid_own,
    hid_oth,
    gf_own,
    gf_oth,
    keep_p,
    send_p,
    keep_q,
    send_q,
    turned,
    tile,
    down,
):
    step = pl.program_id(0)
    rows = 2 * SLOT

    @pl.when(step == 0)
    def _():
        turned[:, :rows] = own_ref[...].T
        turned[:, rows:] = oth_ref[...].T

    @pl.when(step < 8)
    def _():
        tile[...] = (
            dot(turned[:, :rows], g_own[...]) + dot(turned[:, rows:], g_oth[...])
        ).astype(BF16)

    row_to = pl.multiple_of((step % 4) * 96, 16)

    @pl.when(step < 4)
    def _():
        spread(info, tile, 48, 0, 48, 2, masks_p, keep_p, send_p, row_to)

    @pl.when((step >= 4) & (step < 8))
    def _():
        spread(info, tile, 48, 0, 48, 2, masks_q, keep_q, send_q, row_to)

    @pl.when(step >= 8)
    def _():
        at = pl.multiple_of((step - 8) * FBLOCK, FBLOCK)
        down[pl.ds(at, FBLOCK), :] = (
            dot_tn(hid_own[...], gf_own[...]) + dot_tn(hid_oth[...], gf_oth[...])
        ).astype(BF16)

    @pl.when(step == 11)
    def _():
        spread(info, down, 128, 0, 64, 3, masks_p, keep_p, send_p, 384)
        spread(info, down, 128, 64, 64, 3, masks_q, keep_q, send_q, 384)


def feed_weight(info, masks, own, oth, g_own, g_oth, hid_own, hid_oth, gf_own, gf_oth, rows_of, after=()):
    rows = 2 * SLOT
    whole = lambda j, info: (0, 0)
    full = pl.BlockSpec((rows, D), whole)
    grad = pl.BlockSpec((rows, 256), lambda j, info: (0, jnp.minimum(j, 7)))
    hid = pl.BlockSpec((rows, FBLOCK), lambda j, info: (0, jnp.maximum(j - 8, 0)))
    out = pl.BlockSpec((8, 576, LANES), lambda j, info: (0, 0, 0))
    return launch(
        functools.partial(feed_weight_kernel, *masks),
        (info,),
        (12,),
        (own, oth, g_own, g_oth, hid_own, hid_oth, gf_own, gf_oth,),
        [
                full,
                full,
                grad,
                grad,
                hid,
                hid,
                pl.BlockSpec((rows, HALF), lambda j, info: (info[rows_of[0]], info[1])),
                pl.BlockSpec((rows, HALF), lambda j, info: (info[rows_of[1]], info[1])),
            ],
        [shape(8, 576, LANES)] * 4,
        [out] * 4,
        cost(2 * rows * D * 3 * FF, 20e6),
        [
                pltpu.VMEM((D, 2 * rows), BF16),
                pltpu.VMEM((D, 256), BF16),
                pltpu.VMEM((FF, HALF), BF16),
            ],
        after,
    )


def attention_weight_kernel(
    masks_p, masks_q, info, own_ref, oth_ref, g_own, g_oth, keep_p, send_p, keep_q, send_q, turned, tile
):
    step = pl.program_id(0)
    rows = 2 * SLOT

    @pl.when(step == 0)
    def _():
        turned[:, :rows] = own_ref[:, D:].T
        turned[:, rows:] = oth_ref[:, D:].T

    @pl.when(step == 1)
    def _():
        turned[:, :rows] = own_ref[:, :D].T
        turned[:, rows:] = oth_ref[:, :D].T

    tile[...] = (
        dot(turned[:, :rows], g_own[...]) + dot(turned[:, rows:], g_oth[...])
    ).astype(BF16)
    for at, (masks, keep, send, row_to) in enumerate(
        (
            (masks_q, keep_q, send_q, 144),
            (masks_p, keep_p, send_p, 0),
            (masks_p, keep_p, send_p, 144),
            (masks_q, keep_q, send_q, 0),
        )
    ):

        @pl.when(step == at)
        def _():
            spread(info, tile, 48, 0, 48, 3, masks, keep, send, row_to)


def attention_weight(info, masks, own, oth, g_own, g_oth, after=()):
    rows = 2 * SLOT
    whole = lambda j, info: (0, 0)
    full = pl.BlockSpec((rows, 2 * D), whole)
    grad = pl.BlockSpec((rows, HALF), lambda j, info: (0, j))
    out = pl.BlockSpec((8, 288, LANES), lambda j, info: (0, 0, 0))
    return launch(
        functools.partial(attention_weight_kernel, *masks),
        (info,),
        (4,),
        (own, oth, g_own, g_oth,),
        [full, full, grad, grad],
        [shape(8, 288, LANES)] * 4,
        [out] * 4,
        cost(2 * rows * D * 4 * D, 14e6),
        [pltpu.VMEM((D, 2 * rows), BF16), pltpu.VMEM((D, HALF), BF16)],
        after,
    )


def gather(own, order, count):
    have = own[None]
    for bit in order[:-1]:
        have = jnp.concatenate([have, flip(have, bit, count)], axis=0)
    return have, flip(have, order[-1], count)


def place_kernel(plan, n_src, info, *refs):
    srcs, outs, sem = refs[: 4 * n_src], refs[4 * n_src : -1], refs[-1]
    per_layer = len(outs) // 2

    def copies(first, side):
        found = []
        for n, (masks, pieces) in enumerate(plan):
            for place, mask in enumerate(masks):
                src = srcs[4 * n + 2 * side + place // 8]
                shard = info[0] ^ mask
                for row_from, rows, matrix, stride, offset in pieces:
                    at = pl.multiple_of(shard * stride + offset, 16)
                    found.append(
                        pltpu.make_async_copy(
                            src.at[place % 8, row_from : row_from + rows],
                            outs[first * per_layer + matrix].at[pl.ds(at, rows)],
                            sem,
                        )
                    )
        return found

    for section in range(2):

        @pl.when(info[1] == section)
        def _():
            for side in range(2):
                for copy in copies(section ^ side, side):
                    copy.start()

    for side in range(2):
        for copy in copies(side, side):
            copy.wait()


def place(info, plan, sources, dims, after=()):
    flat = [piece for source in sources for piece in source]
    anywhere = pl.BlockSpec(memory_space=pl.ANY)
    outs = launch(
        functools.partial(place_kernel, plan, len(sources)),
        (info,),
        (1,),
        (*flat,),
        [anywhere] * len(flat),
        [shape(*d) for d in dims] * 2,
        [pl.BlockSpec(d, lambda i, info: (0, 0)) for d in dims] * 2,
        cost(0, 4 * 2 * sum(a * b for a, b in dims)),
        [pltpu.SemaphoreType.DMA],
        after,
    )
    return outs[: len(dims)], outs[len(dims) :]


def gather_all(info, shards, count):
    w_q, w_k, w_v, w_o, w_g, w_u, w_d = shards
    half = w_d.shape[0] // 2
    row = w_q.shape[0]
    owns = (
        jnp.concatenate([w_q, w_k], axis=0),
        jnp.concatenate([w_v, w_o], axis=0),
        w_g,
        w_u,
        w_d[:half],
        w_d[half:],
    )
    found = []
    for own, order in zip(owns, GATHER_ORDERS):
        have, last = gather(own, order, count)
        found.append((have, last, swap(have), swap(last)))
    masks = [order_masks(order) for order in GATHER_ORDERS]
    pair = lambda a, b: ((0, row, a, row, 0), (row, row, b, row, 0))
    plan = ((masks[0], pair(0, 1)), (masks[1], pair(2, 3)))
    first = place(info, plan, found[0:2], ((D, D),) * 4)
    plan = ((masks[2], ((0, row, 0, row, 0),)), (masks[3], ((0, row, 1, row, 0),)))
    second = place(info, plan, found[2:4], ((D, FF),) * 2)
    plan = (
        (masks[4], ((0, half, 0, 2 * half, 0),)),
        (masks[5], ((0, half, 0, 2 * half, half),)),
    )
    third = place(info, plan, found[4:6], ((FF, D),))
    return tuple(tuple(first[n]) + tuple(second[n]) + tuple(third[n]) for n in range(2))


def gather_plain(section, shards):
    mine = [lax.all_gather(s, "dp", axis=0, tiled=True) for s in shards]
    theirs = [swap(m) for m in mine]
    low = tuple(jnp.where(section == 0, m, t) for m, t in zip(mine, theirs))
    high = tuple(jnp.where(section == 0, t, m) for m, t in zip(mine, theirs))
    return low, high


def scatter(keep, send, order, count):
    parts = [keep]
    for stage, bit in enumerate(order):
        parts.append(flip(send, bit, count))
        size = 8 >> stage
        if size == 1:
            break
        lower = size // 2
        send = sum(p[lower:size].astype(F32) for p in parts).astype(BF16)
    return sum(p[0].astype(F32) for p in parts)


def unpack_kernel(plan, gained, info, *refs):
    n_src = 1 + max(p[0] for p in plan)
    n_gain = len(gained)
    srcs, refs = refs[: 2 * n_src], refs[2 * n_src :]
    gain, weights, outs = refs[0], refs[1 : 1 + n_gain], refs[1 + n_gain :]
    for section in range(2):

        @pl.when(info[1] == section)
        def _():
            total = jnp.zeros((gain.shape[0], 1), F32)
            for n, (src, row_from, rows, row_to, scale, has_gain, out) in enumerate(plan):
                for side in range(2):
                    piece = srcs[2 * src + (section ^ side)]
                    width = outs[out].shape[1] // 2
                    for block in range(width // LANES):
                        at = row_from + block * rows
                        value = piece[at : at + rows, :]
                        col = side * width + block * LANES
                        if has_gain:
                            weight = weights[gained.index(n)][:, col : col + LANES].astype(F32)
                            total += scale * jnp.sum(weight * value, axis=1, keepdims=True)
                            value = value * (gain[...] * scale)
                        outs[out][row_to : row_to + rows, col : col + LANES] = value
            outs[-1][...] = jnp.broadcast_to(total, outs[-1].shape)


def unpack_all(info, plan, sources, gain, weights, dims, after=()):
    gained = tuple(n for n, p in enumerate(plan) if p[5])
    flat = [piece for source in sources for piece in source]
    return launch(
        functools.partial(unpack_kernel, plan, gained),
        (info,),
        (1,),
        (*flat, gain, *weights,),
        [pl.BlockSpec(v.shape, lambda i, info: (0, 0)) for v in (*flat, gain, *weights)],
        [shape(*d, dtype=F32) for d in dims],
        [pl.BlockSpec(d, lambda i, info: (0, 0)) for d in dims],
        cost(0, 8 * sum(a * b for a, b in dims)),
        (),
        after,
    )


def halves(section, first, second):
    mine = jnp.where(section == 0, first, second)
    return mine, swap(jnp.where(section == 0, second, first))


def on_device(
    tokens,
    heights,
    out_grad,
    w_query,
    w_key,
    w_value,
    w_out,
    w_gate,
    w_up,
    w_down,
    gain_attn,
    gain_ffn,
):
    section = lax.axis_index("section")
    me = lax.axis_index("dp")
    count = lax.axis_size("dp")
    halving = count == 16
    info = jnp.stack([me, section, 1 - section, jnp.zeros_like(me)]).astype(jnp.int32)
    own_rows, oth_rows, no_rows = 1, 2, 3
    lim = WIDE * heights + 1
    gain_one = gain_attn[0].astype(F32)[:, None]
    gain_two = gain_ffn[0].astype(F32)[:, None]
    fold = lambda w, g: (w[0].astype(F32) * g).astype(BF16)
    shards = (
        fold(w_query, gain_one * SCALE),
        fold(w_key, gain_one),
        fold(w_value, gain_one),
        w_out[0],
        fold(w_gate, gain_two),
        fold(w_up, gain_two),
        w_down[0],
    )
    if halving:
        layers = gather_all(info, shards, count)
    else:
        layers = gather_plain(section, shards)
    tables = tuple(jnp.asarray(t) for t in rope_consts())
    rows = 2 * SLOT
    slots = jnp.arange(SLOT)
    valid = (slots[None, :] < lim[:, None]).reshape(-1, 1)
    grad = jnp.where(valid, out_grad, jnp.zeros_like(out_grad))

    kept = []
    x, x_rows = tokens, own_rows
    for layer, (w_q, w_k, w_v, w_o, w_g, w_u, w_d) in enumerate(layers):
        act, qkv, probs, scale_one = attention(info, lim, x, x_rows, w_q, w_k, w_v, tables)
        middle, normed, scale_two, hidden, s1, s2 = feed(info, x, x_rows, act, w_o, w_g, w_u)
        others = (swap(act), swap(normed), swap(hidden))
        kept.append((act, qkv, probs, scale_one, normed, scale_two, hidden, s1, s2, others))
        if layer == 0:
            first = leave(info, lim, middle, hidden, w_d)
            x, x_rows = first, no_rows

    masks = tuple(order_masks(order[::-1]) for order in SCATTER_ORDERS)
    grad_own, grad_oth, grad_rows, oth_at = grad, grad, own_rows, oth_rows
    sums = [None, None]
    gins = [None, None]
    parts = [None, None]
    pending = None
    for layer in (1, 0):
        w_q, w_k, w_v, w_o, w_g, w_u, w_d = layers[layer]
        act, qkv, probs, scale_one, normed, scale_two, hidden, s1, s2, others = kept[layer]
        act_oth, normed_oth, hidden_oth = others
        keep, send, gmid, gz, gmix = feed_back(
            info, grad_own, grad_rows, w_d, w_g, w_u, s1, s2, normed, scale_two, w_o
        )
        recv = swap(send)
        earlier = (send,)
        if layer == 1:
            second = leave(info, lim, middle, hidden, w_d, after=earlier)
            earlier = (second,)
        elif halving:
            pending = attention_weight(info, masks, *parts[1], after=earlier)
            earlier = (pending[1],)
        if halving:
            formed = feed_weight(
                info,
                masks,
                normed,
                normed_oth,
                keep,
                recv,
                hidden,
                hidden_oth,
                grad_own,
                grad_oth,
                (grad_rows, oth_at),
                after=earlier,
            )
            earlier = (formed[1],)
        gin, keep_t, send_t = attention_back(
            info, gmix, qkv, probs, w_q, w_k, w_v, act, scale_one, gmid, gz, tables, after=earlier
        )
        recv_t = swap(send_t)
        gin_oth = swap(gin)
        gins[layer] = (gin, gin_oth)
        parts[layer] = (act, act_oth, keep_t, recv_t)
        if halving:
            kp, sp, kq, sq = formed
            sums[layer] = (
                scatter(kp, sp, SCATTER_ORDERS[0], count),
                scatter(kq, sq, SCATTER_ORDERS[1], count),
            )
        else:
            cut = lambda v, at: lax.dynamic_slice_in_dim(v, at * rows, rows, 0)
            pick = lambda v, at: cut(v, info[at]) if v.shape[0] > rows else v
            gf = jnp.concatenate([pick(grad_own, grad_rows), pick(grad_oth, oth_at)], axis=0)
            gf = lax.dynamic_slice_in_dim(gf, section * HALF, HALF, 1)
            both = lambda a, b: jnp.concatenate([a, b], axis=0)
            form = lambda a, g: lax.psum_scatter(
                lax.dot_general(a, g, (((0,), (0,)), ((), ())), preferred_element_type=F32),
                "dp",
                scatter_dimension=0,
                tiled=True,
            )
            acts, gts = both(act, act_oth), both(keep_t, recv_t)
            gus = both(keep, recv)
            nor = both(normed, normed_oth)
            sums[layer] = (
                form(acts[:, :D], gts[:, HALF : 2 * HALF]),
                form(acts[:, :D], gts[:, 2 * HALF : 3 * HALF]),
                form(acts[:, :D], gts[:, 3 * HALF :]),
                form(acts[:, D:], gts[:, :HALF]),
                form(nor, gus[:, :FHALF]),
                form(nor, gus[:, FHALF:]),
                form(both(hidden, hidden_oth), gf),
            )
        grad_own, grad_oth, grad_rows, oth_at = gin, gin_oth, no_rows, no_rows

    if halving:
        last = attention_weight(info, masks, *parts[0])
        for layer, (kp, sp, kq, sq) in ((1, pending), (0, last)):
            sums[layer] += (
                scatter(kp, sp, SCATTER_ORDERS[0], count),
                scatter(kq, sq, SCATTER_ORDERS[1], count),
            )
    shares = [halves(section, first, second) for first, second in zip(*sums)]
    if halving:
        row, tall = shards[0].shape[0], shards[6].shape[0] // 2
        split, side = row * FHALF // LANES, row * HALF // LANES
        plan = (
            (0, 0, row, 0, 1.0, True, 0),
            (1, 0, row, 0, 1.0, True, 1),
            (0, split, tall, 0, 1.0, False, 2),
            (1, split, tall, tall, 1.0, False, 2),
        )
        grad_g, grad_u, grad_d, gain_grad_two = unpack_all(
            info,
            plan,
            shares[:2],
            gain_two,
            (w_gate[0], w_up[0]),
            ((row, FF), (row, FF), (2 * tall, D), (row, LANES)),
        )
        plan = (
            (0, 0, row, 0, SCALE, True, 0),
            (0, side, row, 0, 1.0, True, 1),
            (1, 0, row, 0, 1.0, True, 2),
            (1, side, row, 0, 1.0, False, 3),
        )
        grad_q, grad_k, grad_v, grad_o, gain_grad_one = unpack_all(
            info,
            plan,
            shares[2:],
            gain_one,
            (w_query[0], w_key[0], w_value[0]),
            ((row, D),) * 4 + ((row, LANES),),
        )
        gain_grad_one, gain_grad_two = gain_grad_one[:, 0], gain_grad_two[:, 0]
    else:

        def cols(pair):
            mine, theirs = pair
            low = jnp.concatenate([mine, theirs], axis=1)
            return jnp.where(section == 0, low, jnp.concatenate([theirs, mine], axis=1))

        grad_q, grad_k, grad_v, grad_o, grad_g, grad_u, grad_d = (cols(s) for s in shares)
        along = lambda w, g: jnp.sum(w[0].astype(F32) * g, axis=1)
        gain_grad_one = SCALE * along(w_query, grad_q)
        gain_grad_one += along(w_key, grad_k) + along(w_value, grad_v)
        gain_grad_two = along(w_gate, grad_g) + along(w_up, grad_u)
        grad_q, grad_k, grad_v = grad_q * (gain_one * SCALE), grad_k * gain_one, grad_v * gain_one
        grad_g, grad_u = grad_g * gain_two, grad_u * gain_two

    def share(first, second, first_oth, second_oth):
        mine = jnp.where(section == 0, first, second)
        theirs = jnp.where(section == 0, first_oth, second_oth)
        return jnp.where(
            section == 0,
            jnp.concatenate([mine, theirs], axis=0),
            jnp.concatenate([theirs, mine], axis=0),
        )[None]

    theirs = swap(jnp.where(section == 0, second, first))
    activations = share(first, second, theirs, theirs)
    input_grads = share(gins[0][0], gins[1][0], gins[0][1], gins[1][1])
    return (
        activations,
        input_grads,
        grad_q[None],
        grad_k[None],
        grad_v[None],
        grad_o[None],
        grad_g[None],
        grad_u[None],
        grad_d[None],
        gain_grad_one[None],
        gain_grad_two[None],
    )


def solution(mesh):
    rows = P("dp", None)
    weight = P("section", "dp", None)
    gain = P("section", "dp")
    return jax.shard_map(
        on_device,
        mesh=mesh,
        in_specs=(rows, P("dp"), rows) + (weight,) * 7 + (gain,) * 2,
        out_specs=(weight,) * 9 + (gain,) * 2,
        check_vma=False,
    )
```

```python
import functools

import jax
import jax.numpy as jnp
import numpy as np
from jax import lax
from jax.experimental import pallas as pl
from jax.experimental.pallas import tpu as pltpu
from jax.sharding import PartitionSpec as P

D = 768
HEADS = 12
HEAD_DIM = 64
FF = 2048
WIDE = 16
SLOT = 256
HALF = D // 2
FHALF = FF // 2
PAIRS = HEADS // 2
LANES = 128
EPS = 1e-05
SCALE = 0.125
F32 = jnp.float32
BF16 = jnp.bfloat16
VMEM_BYTES = 24 * 1024 * 1024

X, Y, ZL, ZH = 1, 2, 4, 8
GATHER = (
    ((ZH, ZL, Y, X), None),
    ((ZH, ZL, X, Y), None),
    ((X, ZH, ZL, Y), None),
    ((ZH, ZL, X, Y), None),
    ((ZL, ZH, X, Y), None),
    ((Y, X, ZH, ZL), None),
)
SCATTER = {
    "D1": (Y, ZH, ZL, X),
    "G1": (X, Y, ZL, ZH),
    "T1": (Y, ZL, X, ZH),
    "D0": (X, Y, ZL, ZH),
    "G0": (Y, X, ZL, ZH),
    "T0": (Y, ZL, X, ZH),
}
ORDER = (
    "g50", "g20", "g00", "g10", "g21", "g01", "g11", "g30", "g51", "g02", "g12", "g31", "g40",
    "g03", "g22", "g13", "g41", "v0", "g42", "w0", "g52", "g32", "w1", "g43", "v1", "g33", "g23",
    "A0", "v2", "w3", "F0", "xa0", "g53", "w2", "w4", "w5", "v3", "dw2", "dw3", "L0", "v4", "A1",
    "v5", "F1", "B1", "xf1", "xs1", "K1", "D1", "xf0", "rD10", "xt1", "G1", "rD11", "xa1", "rG10",
    "B0", "dxa0", "xs0", "T1", "rG11", "rT10", "K0", "G0", "rD12", "rG12", "rT11", "rG00", "xt0",
    "L1", "T0", "rT00", "oi", "rG01", "rT12", "oa", "rG13", "rD13", "rT01", "D0", "rD00", "zG1",
    "rT13", "doa", "rG02", "rT02", "ob", "rD01", "rG03", "rT03", "zT1", "rD02", "zD1", "zG0", "hG",
    "rD03", "zT0", "hT", "zD0", "dhG", "hD", "u2", "u1",
)


def order_masks(order):
    masks = [0]
    for bit in order:
        masks = masks + [m ^ bit for m in masks]
    return masks


def mirrored(order):
    return tuple({X: Y, Y: X}.get(bit, bit) for bit in order)


def flip(value, bit, count, other=None):
    if other is None or other == bit:
        return lax.ppermute(value, "dp", [(i, i ^ bit) for i in range(count)])
    pairs = [(i, i ^ bit) for i in range(count)]
    pairs += [(count + i, count + (i ^ other)) for i in range(count)]
    return lax.ppermute(value, ("section", "dp"), pairs)


def swap(value):
    return lax.ppermute(value, "section", [(0, 1), (1, 0)])


def rope_consts():
    position = np.arange(SLOT)
    index = np.maximum(position - 1, 0)
    started = (position > 0).astype(np.float32)
    row_pos = (index // WIDE).astype(np.float32) * started
    col_pos = (index % WIDE).astype(np.float32) * started
    quarter = HEAD_DIM // 4
    freq = np.power(np.float32(10000.0), -np.arange(quarter, dtype=np.float32) / quarter)
    row_angle = row_pos[:, None] * freq[None, :]
    col_angle = col_pos[:, None] * freq[None, :]
    angle = np.concatenate([row_angle, row_angle, col_angle, col_angle], axis=1)
    angle = np.concatenate([angle, angle], axis=1).astype(np.float32)
    even = (np.arange(LANES) // quarter) % 2 == 0
    sine = np.sin(angle)
    return (
        np.cos(angle).astype(np.float32),
        np.where(even, -sine, 0.0).astype(np.float32),
        np.where(even, 0.0, sine).astype(np.float32),
    )


def dot(left, right):
    return jnp.dot(left, right, preferred_element_type=F32)


def dot_nt(left, right):
    return lax.dot_general(left, right, (((1,), (1,)), ((), ())), preferred_element_type=F32)


def dot_tn(left, right):
    return lax.dot_general(left, right, (((0,), (0,)), ((), ())), preferred_element_type=F32)


def turn(value, sin_a, sin_b):
    return pltpu.roll(value, LANES - 16, 1) * sin_a + pltpu.roll(value, 16, 1) * sin_b


def params(steps=1):
    return pltpu.CompilerParams(
        dimension_semantics=("arbitrary",) * steps, vmem_limit_bytes=VMEM_BYTES
    )


def cost(flops, nbytes):
    return pl.CostEstimate(flops=1, bytes_accessed=1, transcendentals=0)


def shape(*dims, dtype=BF16):
    return jax.ShapeDtypeStruct(dims, dtype)


def kept(*dims, dtype=BF16):
    return pltpu.HBM(dims, dtype)


def far(*arrays):
    return tuple(pltpu.with_memory_space_constraint(a, pltpu.HBM) for a in arrays)


def launch(kernel, prefetch, grid, inputs, in_specs, out_shape, out_specs, work, scratch=()):
    return pl.pallas_call(
        kernel,
        grid_spec=pltpu.PrefetchScalarGridSpec(
            num_scalar_prefetch=len(prefetch),
            grid=grid,
            in_specs=list(in_specs),
            out_specs=out_specs,
            scratch_shapes=list(scratch),
        ),
        out_shape=out_shape,
        compiler_params=params(len(grid)),
        cost_estimate=work,
    )(*prefetch, *inputs)


def head_split(pair):
    lane = lax.broadcasted_iota(jnp.int32, pair.shape, 1)
    zero = jnp.zeros_like(pair)
    return jnp.where(lane < HEAD_DIM, pair, zero), jnp.where(lane < HEAD_DIM, zero, pair)


class Gathered:
    def __init__(self, sources, dims, masks=None, pieces=None):
        self.sources, self.dims, self.masks, self.pieces = tuple(sources), dims, masks, pieces

    def load(self, info, srcs, mats):
        if self.masks is None:
            for src, mat in zip(srcs, mats):
                mat[...] = src[...]
            return
        for section in range(2):

            @pl.when(info[1] == section)
            def _():
                for side in range(2):
                    part = section ^ side
                    for at, mask in enumerate(self.masks[part]):
                        src, shard = srcs[2 * side + at // 8], info[0] ^ mask
                        for row_from, rows, matrix, rest in self.pieces[part]:
                            mats[matrix][(shard, *rest)] = src[at % 8, row_from : row_from + rows]

    def scratch(self):
        kinds = [pltpu.VMEM(d, BF16) for d in self.dims]
        return kinds + [pltpu.SemaphoreType.DMA((len(self.dims),))]


def matrix(ref, rows=None, cols=slice(None)):
    if rows is not None:
        n, count = rows
        size = ref.shape[0] // count
        value = ref[pl.ds(pl.multiple_of(n * size, size), size)]
    else:
        value = ref[(slice(None),) * (len(ref.shape) - 1) + (cols,)]
    return value.reshape(-1, value.shape[-1])


ANYWHERE = pl.BlockSpec(memory_space=pl.ANY)


def loaded(gathered, kernel, n_in, n_out, info, *refs):
    n_src, n_mat = len(gathered.sources), len(gathered.dims)
    ins, srcs, refs = refs[:n_in], refs[n_in : n_in + n_src], refs[n_in + n_src :]
    outs, wholes, refs = refs[:n_out], refs[n_out : n_out + n_mat], refs[n_out + n_mat :]
    mats, out_sems, refs = refs[:n_mat], refs[n_mat], refs[n_mat + 1 :]
    step = pl.program_id(0)
    back = [
        pltpu.make_async_copy(mat, whole, out_sems.at[n])
        for n, (mat, whole) in enumerate(zip(mats, wholes))
    ]

    @pl.when(step == 0)
    def _():
        gathered.load(info, srcs, mats)
        for copy in back:
            copy.start()

    kernel(info, *ins, *mats, *outs, *refs)

    @pl.when(step == pl.num_programs(0) - 1)
    def _():
        for copy in back:
            copy.wait()


def launch_loaded(
    gathered, kernel, prefetch, grid, inputs, in_specs, out_shape, out_specs, work, scratch=()
):
    n_in = len(prefetch) - 1 + len(inputs)
    return launch(
        functools.partial(loaded, gathered, kernel, n_in, len(out_shape)),
        prefetch,
        grid,
        (*inputs, *gathered.sources),
        [*in_specs, *[pl.BlockSpec(memory_space=pltpu.VMEM)] * len(gathered.sources)],
        [*out_shape, *[kept(*d) for d in gathered.dims]],
        [*out_specs, *[ANYWHERE] * len(gathered.dims)],
        work,
        [*gathered.scratch(), *scratch],
    )


def attention_kernel(
    info, lim, x_ref, cos, sin_a, sin_b, wq, wk, wv, wo, act_ref, qkv_ref, probs_ref, scale_ref
):
    image = pl.program_id(0)
    x = x_ref[...].astype(F32)
    r = lax.rsqrt(jnp.mean(x * x, axis=1, keepdims=True) + EPS)
    normed = (x * r).astype(BF16)
    act_ref[:, :D] = normed
    scale_ref[...] = jnp.broadcast_to(r, (SLOT, LANES))
    for part, weight in enumerate((wq, wk)):
        full = dot(normed, matrix(weight))
        for p in range(PAIRS):
            piece = full[:, p * LANES : (p + 1) * LANES]
            piece = piece * cos[...] + turn(piece, sin_a[...], sin_b[...])
            start = part * D + p * LANES
            qkv_ref[:, start : start + LANES] = piece.astype(BF16)
    qkv_ref[:, 2 * D :] = dot(normed, matrix(wv)).astype(BF16)
    row = lax.broadcasted_iota(jnp.int32, (SLOT, SLOT), 0)
    col = lax.broadcasted_iota(jnp.int32, (SLOT, SLOT), 1)
    mask = (col <= row) & (col < lim[info[1] * 2 + image])
    for p in range(PAIRS):
        lanes = slice(p * LANES, (p + 1) * LANES)
        query = qkv_ref[:, lanes]
        keys = head_split(qkv_ref[:, D + p * LANES : D + (p + 1) * LANES])
        values = head_split(qkv_ref[:, 2 * D + p * LANES : 2 * D + (p + 1) * LANES])
        probs = []
        for h in range(2):
            scores = jnp.where(mask, dot_nt(query, keys[h]), -1e30)
            top = jnp.max(scores, axis=1, keepdims=True)
            raised = jnp.exp(scores - top)
            total = jnp.sum(raised, axis=1, keepdims=True)
            probs.append((raised * (1.0 / total)).astype(BF16))
            probs_ref[0, 2 * p + h] = probs[h]
        mixed = dot(jnp.concatenate(probs, axis=1), jnp.concatenate(values, axis=0))
        act_ref[:, D + p * LANES : D + (p + 1) * LANES] = mixed.astype(BF16)


def attention(info, lim, x, x_rows, gathered, tables):
    table = pl.BlockSpec((SLOT, LANES), lambda i, info, lim: (0, 0))
    return launch_loaded(
        gathered,
        attention_kernel,
        (info, lim),
        (2,),
        (x, *tables),
        [
            pl.BlockSpec((SLOT, D), lambda i, info, lim: (info[x_rows] * 2 + i, 0)),
            table,
            table,
            table,
        ],
        [
            shape(2 * SLOT, 2 * D),
            kept(2 * SLOT, 3 * D),
            kept(2, HEADS, SLOT, SLOT),
            kept(2 * SLOT, LANES, dtype=F32),
        ],
        [
            pl.BlockSpec((SLOT, 2 * D), lambda i, info, lim: (i, 0)),
            pl.BlockSpec((SLOT, 3 * D), lambda i, info, lim: (i, 0)),
            pl.BlockSpec((1, HEADS, SLOT, SLOT), lambda i, info, lim: (i, 0, 0, 0)),
            pl.BlockSpec((SLOT, LANES), lambda i, info, lim: (i, 0)),
        ],
        cost(3.6e9 + 24 * 4 * 256 * 256 * 128, 12e6),
    )


FBLOCK = 512


PACK = 1024


def feed_kernel(info, x_ref, mixed_ref, wo, wg, wu, middle_ref, scale_ref, pack_ref, s1_ref, s2_ref, normed):
    step = pl.program_id(0)
    lead = PACK // FBLOCK

    @pl.when(step == 0)
    def _():
        middle = x_ref[...].astype(F32) + dot(mixed_ref[...], wo[...])
        r = lax.rsqrt(jnp.mean(middle * middle, axis=1, keepdims=True) + EPS)
        middle_ref[...] = middle
        scale_ref[...] = jnp.broadcast_to(r, scale_ref.shape)
        normed[:, :D] = (middle * r).astype(BF16)
        normed[:, D:] = jnp.zeros((normed.shape[0], PACK - D), BF16)

    for part in range(lead):

        @pl.when(step == part)
        def _():
            pack_ref[...] = normed[:, part * FBLOCK : (part + 1) * FBLOCK]

    @pl.when(step >= lead)
    def _():
        cols = pl.ds(pl.multiple_of((step - lead) * FBLOCK, FBLOCK), FBLOCK)
        gate = dot(normed[:, :D], matrix(wg, cols=cols))
        up = dot(normed[:, :D], matrix(wu, cols=cols))
        sig = 0.5 * jnp.tanh(0.5 * gate) + 0.5
        silu = gate * sig
        pack_ref[...] = (silu * up).astype(BF16)
        s1_ref[...] = (up * (sig * (1.0 + gate * (1.0 - sig)))).astype(BF16)
        s2_ref[...] = silu.astype(BF16)


def feed(info, x, x_rows, act, wo, gathered):
    rows = 2 * SLOT
    lead = PACK // FBLOCK
    whole = lambda j, info: (0, 0)
    wide = pl.BlockSpec((rows, FBLOCK), lambda j, info: (0, jnp.maximum(j - lead, 0)))
    return launch_loaded(
        gathered,
        feed_kernel,
        (info,),
        (lead + FF // FBLOCK,),
        (x, act, wo),
        [
            pl.BlockSpec((rows, D), lambda j, info: (info[x_rows], 0)),
            pl.BlockSpec((rows, D), lambda j, info: (0, 1)),
            pl.BlockSpec((D, D), whole),
        ],
        [
            shape(rows, D, dtype=F32),
            kept(rows, LANES, dtype=F32),
            shape(rows, PACK + FF),
            kept(rows, FF),
            kept(rows, FF),
        ],
        [
            pl.BlockSpec((rows, D), whole),
            pl.BlockSpec((rows, LANES), whole),
            pl.BlockSpec((rows, FBLOCK), lambda j, info: (0, j)),
            wide,
            wide,
        ],
        cost(2 * rows * D * (D + 2 * FF), 18e6),
        [pltpu.VMEM((rows, PACK), BF16)],
    )


def leave_kernel(info, lim, middle_ref, low, high, wd, out_ref):
    image = pl.program_id(0)
    result = middle_ref[...] + dot(low[...], matrix(wd, (0, 2))) + dot(high[...], matrix(wd, (1, 2)))
    row = lax.broadcasted_iota(jnp.int32, result.shape, 0)
    out_ref[...] = jnp.where(row < lim[info[1] * 2 + image], result, 0.0).astype(BF16)


def leave(info, lim, middle, pack, wd):
    rows = 2 * SLOT
    args = (
        (info, lim),
        (2,),
        (middle, pack, pack),
        [
            pl.BlockSpec((SLOT, D), lambda i, info, lim: (i, 0)),
            pl.BlockSpec((SLOT, PACK), lambda i, info, lim: (i, 1)),
            pl.BlockSpec((SLOT, PACK), lambda i, info, lim: (i, 2)),
        ],
        [shape(rows, D)],
        [pl.BlockSpec((SLOT, D), lambda i, info, lim: (i, 0))],
        cost(2 * rows * D * FF, 8e6),
    )
    if isinstance(wd, Gathered):
        return launch_loaded(wd, leave_kernel, *args)
    prefetch, grid, inputs, in_specs, *rest = args
    in_specs = [*in_specs, pl.BlockSpec((FF, D), lambda i, info, lim: (0, 0))]
    return launch(leave_kernel, prefetch, grid, (*inputs, wd), in_specs, *rest)


def feed_back_kernel(
    info,
    grad_ref,
    wg,
    wu,
    s1_ref,
    s2_ref,
    normed_ref,
    scale_ref,
    wo,
    wd,
    keep_ref,
    send_ref,
    gmid_ref,
    gz_ref,
    gmix_ref,
    total,
):
    step = pl.program_id(0)
    per_half = FHALF // FBLOCK
    down = wd[...] if wd.shape[0] == FBLOCK else matrix(wd, (step, FF // FBLOCK))
    grad_hidden = dot_nt(grad_ref[...], down)
    ggate = (grad_hidden * s1_ref[...].astype(F32)).astype(BF16)
    gup = (grad_hidden * s2_ref[...].astype(F32)).astype(BF16)
    at = pl.multiple_of((step % per_half) * FBLOCK, FBLOCK)
    own = (step // per_half) == info[1]

    @pl.when(own)
    def _():
        keep_ref[:, pl.ds(at, FBLOCK)] = ggate
        keep_ref[:, pl.ds(at + FHALF, FBLOCK)] = gup

    @pl.when(jnp.logical_not(own))
    def _():
        send_ref[:, pl.ds(at, FBLOCK)] = ggate
        send_ref[:, pl.ds(at + FHALF, FBLOCK)] = gup

    part = dot_nt(ggate, wg[...]) + dot_nt(gup, wu[...])

    @pl.when(step == 0)
    def _():
        total[...] = part

    @pl.when(step > 0)
    def _():
        total[...] += part

    @pl.when(step == pl.num_programs(0) - 1)
    def _():
        gn = total[...]
        normed = normed_ref[...].astype(F32)
        mean = jnp.mean(gn * normed, axis=1, keepdims=True)
        gmid = grad_ref[...].astype(F32) + scale_ref[:, :1] * (gn - normed * mean)
        gz = gmid.astype(BF16)
        gmid_ref[...] = gmid
        gz_ref[...] = gz
        gmix_ref[...] = dot_nt(gz, wo[...]).astype(BF16)


def feed_back(info, grad, grad_rows, wd, wg, wu, s1, s2, pack, scale, wo):
    rows = 2 * SLOT
    whole = lambda j, info: (0, 0)
    col = pl.BlockSpec((D, FBLOCK), lambda j, info: (0, j))
    wide = pl.BlockSpec((rows, FBLOCK), lambda j, info: (0, j))
    full = pl.BlockSpec((rows, D), whole)
    args = (
        (info,),
        (FF // FBLOCK,),
        (grad, *far(wg, wu, s1, s2), pack, *far(scale, wo)),
        [
            pl.BlockSpec((rows, D), lambda j, info: (info[grad_rows], 0)),
            col,
            col,
            wide,
            wide,
            full,
            pl.BlockSpec((rows, LANES), whole),
            pl.BlockSpec((D, D), whole),
        ],
        [
            shape(rows, FF),
            shape(rows, FF),
            shape(rows, D, dtype=F32),
            shape(rows, D),
            shape(rows, D),
        ],
        [
            pl.BlockSpec((rows, FF), whole),
            pl.BlockSpec((rows, FF), whole),
            full,
            full,
            full,
        ],
        cost(2 * rows * D * (3 * FF + D), 24e6),
        [pltpu.VMEM((rows, D), F32)],
    )
    if isinstance(wd, Gathered):
        return launch_loaded(wd, feed_back_kernel, *args)
    prefetch, grid, inputs, in_specs, *rest = args
    in_specs = [*in_specs, pl.BlockSpec((FBLOCK, D), lambda j, info: (j, 0))]
    return launch(feed_back_kernel, prefetch, grid, (*inputs, *far(wd)), in_specs, *rest)


def attention_back_kernel(
    info,
    gmix_ref,
    qkv_ref,
    probs_ref,
    wq,
    wk,
    wv,
    normed_ref,
    scale_ref,
    gmid_ref,
    gz_ref,
    cos,
    sin_a,
    sin_b,
    gin_ref,
    keep_ref,
    send_ref,
    grads,
):
    for p in range(PAIRS):
        lanes = slice(p * LANES, (p + 1) * LANES)
        gmix = gmix_ref[:, lanes]
        query = head_split(qkv_ref[:, lanes])
        keys = head_split(qkv_ref[:, D + p * LANES : D + (p + 1) * LANES])
        values = head_split(qkv_ref[:, 2 * D + p * LANES : 2 * D + (p + 1) * LANES])
        gmix_parts = head_split(gmix)
        gs_parts = []
        for h in range(2):
            probs = probs_ref[0, 2 * p + h].astype(F32)
            weighted = probs * dot_nt(gmix, values[h])
            inner = jnp.sum(weighted, axis=1, keepdims=True)
            gs_parts.append((weighted - probs * inner).astype(BF16))
        gq = dot(jnp.concatenate(gs_parts, axis=1), jnp.concatenate(keys, axis=0))
        gk = dot_tn(gs_parts[0], query[0]) + dot_tn(gs_parts[1], query[1])
        gv = dot_tn(probs_ref[0, 2 * p], gmix_parts[0]) + dot_tn(
            probs_ref[0, 2 * p + 1], gmix_parts[1]
        )
        gq = gq * cos[...] - turn(gq, sin_a[...], sin_b[...])
        gk = gk * cos[...] - turn(gk, sin_a[...], sin_b[...])
        grads[0, :, lanes] = gq.astype(BF16)
        grads[1, :, lanes] = gk.astype(BF16)
        grads[2, :, lanes] = gv.astype(BF16)
    gn = dot_nt(grads[0], wq[...]) + dot_nt(grads[1], wk[...]) + dot_nt(grads[2], wv[...])
    normed = normed_ref[...].astype(F32)
    mean = jnp.mean(gn * normed, axis=1, keepdims=True)
    gin = gmid_ref[...] + scale_ref[:, :1] * (gn - normed * mean)
    gin_ref[...] = gin.astype(BF16)
    send_ref[:, 4 * HALF :] = gin.astype(BF16)
    for h in range(2):

        @pl.when(info[1] == h)
        def _():
            for out, half in ((keep_ref, h), (send_ref, 1 - h)):
                cols = slice(half * HALF, (half + 1) * HALF)
                out[:, :HALF] = gz_ref[:, cols]
                for part in range(3):
                    out[:, (part + 1) * HALF : (part + 2) * HALF] = grads[part, :, cols]


def attention_back(info, gmix, qkv, probs, wq, wk, wv, act, scale, gmid, gz, tables):
    rows = 2 * SLOT
    whole = lambda i, info: (0, 0)
    table = pl.BlockSpec((SLOT, LANES), whole)
    weight = pl.BlockSpec((D, D), whole)
    full = pl.BlockSpec((SLOT, D), lambda i, info: (i, 0))
    pack = pl.BlockSpec((SLOT, 4 * HALF), lambda i, info: (i, 0))
    longer = pl.BlockSpec((SLOT, 6 * HALF), lambda i, info: (i, 0))
    return launch(
        attention_back_kernel,
        (info,),
        (2,),
        (gmix, *far(qkv, probs, wq, wk, wv), act, *far(scale), gmid, gz, *tables),
        [
                full,
                pl.BlockSpec((SLOT, 3 * D), lambda i, info: (i, 0)),
                pl.BlockSpec((1, HEADS, SLOT, SLOT), lambda i, info: (i, 0, 0, 0)),
                weight,
                weight,
                weight,
                full,
                pl.BlockSpec((SLOT, LANES), lambda i, info: (i, 0)),
                full,
                full,
                table,
                table,
                table,
            ],
        [shape(rows, D), shape(rows, 4 * HALF), shape(rows, 6 * HALF)],
        [full, pack, longer],
        cost(2 * rows * D * 3 * D + 24 * 8 * 256 * 256 * 128, 16e6),
        [pltpu.VMEM((3, SLOT, D), BF16)],
    )


def spread(info, masks, scratch, rows, lane_blocks, keep, send, row_to):
    for place, (low, high) in enumerate(zip(*masks)):
        shard = info[0] ^ (low + (high - low) * info[1])
        at = pl.multiple_of(shard * rows, 16)
        out = keep if place < 8 else send
        for block in range(lane_blocks):
            out[place % 8, pl.ds(row_to + block * rows, rows), :] = scratch[
                pl.ds(at, rows), block * LANES : (block + 1) * LANES
            ]


def gate_weight_kernel(masks, info, own_ref, oth_ref, g_own, g_oth, keep, send, turned, tile):
    step = pl.program_id(0)
    rows = 2 * SLOT

    @pl.when(step == 0)
    def _():
        turned[:, :rows] = own_ref[...].T
        turned[:, rows:] = oth_ref[...].T

    tile[...] = (
        dot(turned[:, :rows], g_own[...]) + dot(turned[:, rows:], g_oth[...])
    ).astype(BF16)
    spread(info, masks, tile, 48, 4, keep, send, pl.multiple_of(step * 192, 16))


def gate_weight(info, masks, own, oth, g_own, g_oth):
    rows = 2 * SLOT
    full = pl.BlockSpec((rows, D), lambda j, info: (0, 0))
    grad = pl.BlockSpec((rows, 512), lambda j, info: (0, j))
    out = pl.BlockSpec((8, 768, LANES), lambda j, info: (0, 0, 0))
    return launch(
        functools.partial(gate_weight_kernel, masks),
        (info,),
        (4,),
        (own, oth, g_own, g_oth),
        [full, full, grad, grad],
        [shape(8, 768, LANES)] * 2,
        [out] * 2,
        cost(2 * rows * D * 2 * FF, 14e6),
        [pltpu.VMEM((D, 2 * rows), BF16), pltpu.VMEM((D, 512), BF16)],
    )


def down_weight_kernel(masks, info, hid_own, hid_oth, gf_own, gf_oth, keep, send, down):
    step = pl.program_id(0)
    at = pl.multiple_of(step * FBLOCK, FBLOCK)
    down[pl.ds(at, FBLOCK), :] = (
        dot_tn(hid_own[...], gf_own[...]) + dot_tn(hid_oth[...], gf_oth[...])
    ).astype(BF16)

    @pl.when(step == FF // FBLOCK - 1)
    def _():
        spread(info, masks, down, 128, 3, keep, send, 0)


def down_weight(info, masks, pack_own, pack_oth, gf_own, gf_oth, rows_of, col):
    rows = 2 * SLOT
    hid = pl.BlockSpec((rows, FBLOCK), lambda j, info: (0, j + PACK // FBLOCK))
    out = pl.BlockSpec((8, 384, LANES), lambda j, info: (0, 0, 0))
    return launch(
        functools.partial(down_weight_kernel, masks),
        (info,),
        (FF // FBLOCK,),
        (pack_own, pack_oth, gf_own, gf_oth),
        [
            hid,
            hid,
            pl.BlockSpec((rows, HALF), lambda j, info: (info[rows_of[0]], info[1])),
            pl.BlockSpec((rows, HALF), lambda j, info: (info[rows_of[1]], col + info[1])),
        ],
        [shape(8, 384, LANES)] * 2,
        [out] * 2,
        cost(2 * rows * D * FF, 9e6),
        [pltpu.VMEM((FF, HALF), BF16)],
    )


def attention_weight_kernel(masks, info, own_ref, oth_ref, g_own, g_oth, keep, send, turned, tile):
    step = pl.program_id(0)
    rows = 2 * SLOT

    @pl.when(step == 0)
    def _():
        turned[:, :rows] = own_ref[:, D:].T
        turned[:, rows:] = oth_ref[:, D:].T

    @pl.when(step == 1)
    def _():
        turned[:, :rows] = own_ref[:, :D].T
        turned[:, rows:] = oth_ref[:, :D].T

    tile[...] = (
        dot(turned[:, :rows], g_own[...]) + dot(turned[:, rows:], g_oth[...])
    ).astype(BF16)
    spread(info, masks, tile, 48, 3, keep, send, pl.multiple_of(step * 144, 16))


def attention_weight(info, masks, own, oth, g_own, g_oth):
    rows = 2 * SLOT
    full = pl.BlockSpec((rows, 2 * D), lambda j, info: (0, 0))
    grad = pl.BlockSpec((rows, HALF), lambda j, info: (0, j))
    out = pl.BlockSpec((8, 576, LANES), lambda j, info: (0, 0, 0))
    return launch(
        functools.partial(attention_weight_kernel, masks),
        (info,),
        (4,),
        (own, oth, g_own, g_oth),
        [full, full, grad, grad],
        [shape(8, 576, LANES)] * 2,
        [out] * 2,
        cost(2 * rows * D * 4 * D, 14e6),
        [pltpu.VMEM((D, 2 * rows), BF16), pltpu.VMEM((D, HALF), BF16)],
    )


def gather_plain(section, shards):
    mine = [lax.all_gather(s, "dp", axis=0, tiled=True) for s in shards]
    theirs = [swap(m) for m in mine]
    low = tuple(jnp.where(section == 0, m, t) for m, t in zip(mine, theirs))
    high = tuple(jnp.where(section == 0, t, m) for m, t in zip(mine, theirs))
    return low, high


def unpack_kernel(plan, gained, info, *refs):
    n_src = 1 + max(p[0] for p in plan)
    n_gain = len(gained)
    srcs, refs = refs[: 2 * n_src], refs[2 * n_src :]
    gain, weights, outs = refs[0], refs[1 : 1 + n_gain], refs[1 + n_gain :]
    for section in range(2):

        @pl.when(info[1] == section)
        def _():
            total = jnp.zeros((gain.shape[0], 1), F32)
            for n, (src, row_from, rows, row_to, scale, has_gain, out) in enumerate(plan):
                for side in range(2):
                    piece = srcs[2 * src + (section ^ side)]
                    width = outs[out].shape[1] // 2
                    for block in range(width // LANES):
                        at = row_from + block * rows
                        value = piece[at : at + rows, :]
                        col = side * width + block * LANES
                        if has_gain:
                            weight = weights[gained.index(n)][:, col : col + LANES].astype(F32)
                            total += scale * jnp.sum(weight * value, axis=1, keepdims=True)
                            value = value * (gain[...] * scale)
                        outs[out][row_to : row_to + rows, col : col + LANES] = value
            outs[-1][...] = jnp.broadcast_to(total, outs[-1].shape)


def unpack_all(info, plan, sources, gain, weights, dims):
    gained = tuple(n for n, p in enumerate(plan) if p[5])
    flat = [piece for source in sources for piece in source]
    return launch(
        functools.partial(unpack_kernel, plan, gained),
        (info,),
        (1,),
        (*flat, gain, *weights,),
        [pl.BlockSpec(v.shape, lambda i, info: (0, 0)) for v in (*flat, gain, *weights)],
        [shape(*d, dtype=F32) for d in dims],
        [pl.BlockSpec(d, lambda i, info: (0, 0)) for d in dims],
        cost(0, 8 * sum(a * b for a, b in dims)),
        (),
    )


def on_device(
    tokens,
    heights,
    out_grad,
    w_query,
    w_key,
    w_value,
    w_out,
    w_gate,
    w_up,
    w_down,
    gain_attn,
    gain_ffn,
):
    section = lax.axis_index("section")
    me = lax.axis_index("dp")
    count = lax.axis_size("dp")
    halving = count == 16
    rows = 2 * SLOT
    info = jnp.stack([me, section, 1 - section, jnp.zeros_like(me)]).astype(jnp.int32)
    own_rows, oth_rows, no_rows = 1, 2, 3
    token = [info]
    lim = WIDE * heights + 1
    gain_one = gain_attn[0].astype(F32)[:, None]
    gain_two = gain_ffn[0].astype(F32)[:, None]
    fold = lambda w, g: (w[0].astype(F32) * g).astype(BF16)
    shards = (
        fold(w_query, gain_one * SCALE),
        fold(w_key, gain_one),
        fold(w_value, gain_one),
        w_out[0],
        fold(w_gate, gain_two),
        fold(w_up, gain_two),
        w_down[0],
    )
    half, row = shards[6].shape[0] // 2, shards[0].shape[0]
    tables = tuple(jnp.asarray(t) for t in rope_consts())
    slots = jnp.arange(SLOT)
    valid = (slots[None, :] < lim[:, None]).reshape(-1, 1)
    grad = jnp.where(valid, out_grad, jnp.zeros_like(out_grad))

    def tie(*arrays):
        out = lax.optimization_barrier((*arrays, token[0]))
        token[0] = out[-1]
        return out[:-1] if len(arrays) > 1 else out[0]

    env = {}
    have, parts = {}, {}
    pair = lambda a, b: ((0, row, a, ()), (row, row, b, ()))
    pieces = (
        (pair(0, 1), pair(2, 3)),
        (((0, row, 0, ()),), ((0, row, 1, ()),)),
        (((0, half, 0, (0,)),), ((0, half, 0, (1,)),)),
    )
    if halving:
        dims = (((count, row, D),) * 4, ((count, row, FF),) * 2, ((count, 2, half, D),))
    else:
        dims = (((D, D),) * 4, ((D, FF),) * 2, ((FF, D),))
    flat = lambda found: tuple(w.reshape(-1, w.shape[-1]) for w in found)
    wholes, weights = {}, {}
    if halving:
        groups = (
            (jnp.concatenate(shards[0:2], axis=0), jnp.concatenate(shards[2:4], axis=0)),
            (shards[4], shards[5]),
            (shards[6][:half], shards[6][half:]),
        )
        for n, (first, second) in enumerate(groups):
            mine = jnp.where(section == 0, first, second)
            theirs = swap(jnp.where(section == 0, second, first))
            have[n] = jnp.where(section == 0, mine, theirs)[None]
            have[n + 3] = jnp.where(section == 0, theirs, mine)[None]
    else:
        for layer, found in enumerate(gather_plain(section, shards)):
            for group, some in enumerate((found[:4], found[4:6], found[6:])):
                wholes[3 * layer + group] = Gathered(some, dims[group])

    def double(stream, stage):
        order, after = GATHER[stream]
        if stage:
            env["g", stream, stage - 1] = got = tie(env["g", stream, stage - 1])
            have[stream] = jnp.concatenate([have[stream], got], axis=0)
        elif after is not None:
            env[("g",) + after] = tie(env[("g",) + after])
        have[stream] = tie(have[stream])
        env["g", stream, stage] = flip(
            have[stream], order[stage], count, mirrored(order)[stage]
        )

    def gathered(stream):
        if not halving:
            return wholes[stream]
        order = GATHER[stream][0]
        masks = (order_masks(order), order_masks(mirrored(order)))
        theirs, last = tie(env["w", stream], env["v", stream])
        sources = (have[stream], env["g", stream, 3], theirs, last)
        return Gathered(sources, dims[stream % 3], masks, pieces[stream % 3])

    def halve(name, stage):
        order = SCATTER[name]
        if stage:
            parts[name].append(tie(env["r", name, stage - 1]))
            size = 8 >> (stage - 1)
            send = sum(p[size // 2 : size].astype(F32) for p in parts[name]).astype(BF16)
        else:
            parts[name], send = [env[name][0]], env[name][1]
        env["r", name, stage] = flip(tie(send), order[stage], count, mirrored(order)[stage])

    def total(name):
        parts[name].append(tie(env["r", name, 3]))
        env["z", name] = tie(sum(p[0].astype(F32) for p in parts[name]))

    def attend(layer):
        x, x_rows = (tokens, own_rows) if layer == 0 else (env["L", 0], no_rows)
        out = tie(*attention(token[0], lim, x, x_rows, gathered(3 * layer), tables))
        env["A", layer], weights[3 * layer] = out[:4], flat(out[4:])

    def feed_on(layer):
        x, x_rows = (tokens, own_rows) if layer == 0 else (env["L", 0], no_rows)
        w_o, source = weights[3 * layer][3], gathered(3 * layer + 1)
        out = tie(*feed(token[0], x, x_rows, env["A", layer][0], w_o, source))
        env["F", layer], weights[3 * layer + 1] = out[:5], flat(out[5:])

    def leave_off(layer):
        middle, _, pack, _, _ = env["F", layer]
        w_d = gathered(2) if layer == 0 else weights[5][0]
        out = leave(token[0], lim, middle, pack, w_d)
        out = tie(*out) if len(out) > 1 else (tie(*out),)
        env["L", layer] = out[0]
        if layer == 0:
            weights[2] = flat(out[1:])

    def cotangent(layer):
        if layer == 1:
            return grad, grad, own_rows, oth_rows
        return env["K", 1][0], env["xt1"], no_rows, no_rows

    def feed_in(layer):
        own, _, at, _ = cotangent(layer)
        _, scale, pack, s1, s2 = env["F", layer]
        w_g, w_u = weights[3 * layer + 1]
        w_d = gathered(5) if layer == 1 else weights[2][0]
        w_o = weights[3 * layer][3]
        out = tie(*feed_back(token[0], own, at, w_d, w_g, w_u, s1, s2, pack, scale, w_o))
        env["B", layer] = out[:5]
        if layer == 1:
            weights[5] = flat(out[5:])

    def attend_in(layer):
        act, qkv, probs, scale = env["A", layer]
        _, _, gmid, gz, gmix = env["B", layer]
        w = weights[3 * layer][:3]
        env["K", layer] = tie(
            *attention_back(token[0], gmix, qkv, probs, *w, act, scale, gmid, gz, tables)
        )

    def masks_of(name):
        order = SCATTER[name][::-1]
        return order_masks(order), order_masks(mirrored(order))

    def form(name):
        layer = int(name[1])
        if name[0] == "D":
            key, col = "xf%d" % layer, 0
            env[key] = tie(env[key])
            if layer == 0:
                env["xt1"], col = tie(env["xt1"]), 4
            own, oth, at, oth_at = cotangent(layer)
            args = (env["F", layer][2], env[key], own, oth, (at, oth_at), col)
            made = down_weight(token[0], masks_of(name), *args)
        elif name[0] == "G":
            other, recv = tie(env["xf%d" % layer], env["xs%d" % layer])
            args = (env["F", layer][2], other, env["B", layer][0], recv)
            made = gate_weight(token[0], masks_of(name), *args)
        else:
            other, recv = tie(env["xa%d" % layer], env["xt%d" % layer])
            args = (env["A", layer][0], other, env["K", layer][1], recv)
            made = attention_weight(token[0], masks_of(name), *args)
        env[name] = tie(*made)

    sent = {
        "a": lambda layer: env["A", layer][0],
        "f": lambda layer: env["F", layer][2],
        "s": lambda layer: env["B", layer][1],
        "t": lambda layer: env["K", layer][2],
    }

    def both(mine, theirs):
        low = jnp.concatenate([mine, theirs], axis=0)
        return jnp.where(section == 0, low, jnp.concatenate([theirs, mine], axis=0))[None]

    pick = lambda first, second: jnp.where(section == 0, first, second)

    def unpacked(names, plan, gain, local, out_dims):
        sources = [(env["m", n], tie(env["h", n])) for n in names]
        return unpack_all(token[0], plan, sources, gain, local, out_dims)

    def run(name):
        kind, rest = name[0], name[1:]
        if kind == "g":
            double(int(rest[0]), int(rest[1]))
        elif kind == "w":
            env["w", int(rest)] = swap(tie(have[int(rest)]))
        elif kind == "v":
            key = ("g", int(rest), 3)
            env[key] = tie(env[key])
            env["v", int(rest)] = swap(env[key])
        elif kind == "r":
            halve(rest[:2], int(rest[2]))
        elif kind == "z":
            total(rest)
        elif kind == "d":
            kind, rest = rest[0], rest[1:]
            keys = {
                "g": lambda: ("g", int(rest[0]), int(rest[1])),
                "r": lambda: ("r", rest[:2], int(rest[2])),
                "x": lambda: "x" + rest,
                "o": lambda: "o" + rest,
                "h": lambda: ("h", rest),
            }
            key = keys.get(kind, lambda: (kind, int(rest)))()
            env[key] = tie(env[key])
        elif kind == "x":
            env[name] = swap(tie(sent[rest[0]](int(rest[1]))))
        elif kind == "h":
            first, second = env["z", rest + "0"], env["z", rest + "1"]
            env["m", rest], other = tie(pick(first, second), pick(second, first))
            env["h", rest] = swap(other)
        elif name == "u1":
            plan = (
                (0, 0, row, 0, 1.0, True, 0),
                (0, row * FHALF // LANES, row, 0, 1.0, True, 1),
                (1, 0, 2 * half, 0, 1.0, False, 2),
            )
            out_dims = ((row, FF), (row, FF), (2 * half, D), (row, LANES))
            env["u1"] = unpacked("GD", plan, gain_two, (w_gate[0], w_up[0]), out_dims)
        elif name == "u2":
            side = row * HALF // LANES
            plan = (
                (0, side, row, 0, SCALE, True, 0),
                (0, 2 * side, row, 0, 1.0, True, 1),
                (0, 3 * side, row, 0, 1.0, True, 2),
                (0, 0, row, 0, 1.0, False, 3),
            )
            local = (w_query[0], w_key[0], w_value[0])
            out_dims = ((row, D),) * 4 + ((row, LANES),)
            env["u2"] = unpacked("T", plan, gain_one, local, out_dims)
        elif name == "oa":
            env["oa"] = swap(tie(pick(env["L", 1], env["L", 0])))
        elif name == "ob":
            env["ob"] = both(pick(env["L", 0], env["L", 1]), tie(env["oa"]))
        elif name == "oi":
            other = [v[:, 4 * HALF :] for v in tie(env["xt0"], env["xt1"])]
            env["oi"] = both(pick(env["K", 0][0], env["K", 1][0]), pick(*other))
        else:
            layer = int(rest)
            {"A": attend, "F": feed_on, "L": leave_off, "B": feed_in, "K": attend_in}[kind](layer)

    for name in ORDER:
        if name[0] in "DGT":
            if halving:
                form(name)
        elif halving or name[0] in "xoAFLBK":
            run(name)

    if halving:
        grad_g, grad_u, grad_d, gain_grad_two = env["u1"]
        grad_q, grad_k, grad_v, grad_o, gain_grad_one = env["u2"]
        gain_grad_one, gain_grad_two = gain_grad_one[:, 0], gain_grad_two[:, 0]
    else:
        cut = lambda v, at: lax.dynamic_slice_in_dim(v, info[at] * rows, rows, 0)
        join = lambda a, b: jnp.concatenate([a, b], axis=0)

        def reduced(a, g):
            full = lax.dot_general(a, g, (((0,), (0,)), ((), ())), preferred_element_type=F32)
            return lax.psum_scatter(full, "dp", scatter_dimension=0, tiled=True)

        found = []
        for layer in range(2):
            own, oth, at, oth_at = cotangent(layer)
            oth = oth if layer == 1 else oth[:, 4 * HALF :]
            gf = lax.dynamic_slice_in_dim(
                join(cut(own, at), cut(oth, oth_at)), section * HALF, HALF, 1
            )
            acts = join(env["A", layer][0], env["xa%d" % layer])
            gts = join(env["K", layer][1], env["xt%d" % layer][:, : 4 * HALF])
            gus = join(env["B", layer][0], env["xs%d" % layer])
            pack = join(env["F", layer][2], env["xf%d" % layer])
            nor, hid = pack[:, :D], pack[:, PACK:]
            found.append(
                (
                    reduced(acts[:, :D], gts[:, HALF : 2 * HALF]),
                    reduced(acts[:, :D], gts[:, 2 * HALF : 3 * HALF]),
                    reduced(acts[:, :D], gts[:, 3 * HALF :]),
                    reduced(acts[:, D:], gts[:, :HALF]),
                    reduced(nor, gus[:, :FHALF]),
                    reduced(nor, gus[:, FHALF:]),
                    reduced(hid, gf),
                )
            )

        def cols(first, second):
            mine, theirs = pick(first, second), swap(pick(second, first))
            low = jnp.concatenate([mine, theirs], axis=1)
            return pick(low, jnp.concatenate([theirs, mine], axis=1))

        grads = [cols(first, second) for first, second in zip(*found)]
        grad_q, grad_k, grad_v, grad_o, grad_g, grad_u, grad_d = grads
        along = lambda w, g: jnp.sum(w[0].astype(F32) * g, axis=1)
        gain_grad_one = SCALE * along(w_query, grad_q)
        gain_grad_one += along(w_key, grad_k) + along(w_value, grad_v)
        gain_grad_two = along(w_gate, grad_g) + along(w_up, grad_u)
        grad_q, grad_k, grad_v = grad_q * (gain_one * SCALE), grad_k * gain_one, grad_v * gain_one
        grad_g, grad_u = grad_g * gain_two, grad_u * gain_two

    return (
        env["ob"],
        env["oi"],
        grad_q[None],
        grad_k[None],
        grad_v[None],
        grad_o[None],
        grad_g[None],
        grad_u[None],
        grad_d[None],
        gain_grad_one[None],
        gain_grad_two[None],
    )


def solution(mesh):
    rows = P("dp", None)
    weight = P("section", "dp", None)
    gain = P("section", "dp")
    return jax.shard_map(
        on_device,
        mesh=mesh,
        in_specs=(rows, P("dp"), rows) + (weight,) * 7 + (gain,) * 2,
        out_specs=(weight,) * 9 + (gain,) * 2,
        check_vma=False,
    )
```

```python
import functools

import jax
import jax.numpy as jnp
import numpy as np
from jax import lax
from jax.experimental import pallas as pl
from jax.experimental.pallas import tpu as pltpu
from jax.sharding import PartitionSpec as P

D = 768
HEADS = 12
HEAD_DIM = 64
FF = 2048
WIDE = 16
SLOT = 256
HALF = D // 2
FHALF = FF // 2
PAIRS = HEADS // 2
LANES = 128
EPS = 1e-05
SCALE = 0.125
F32 = jnp.float32
BF16 = jnp.bfloat16
VMEM_BYTES = 24 * 1024 * 1024

X, Y, ZL, ZH = 1, 2, 4, 8
GATHER = (
    ((ZH, ZL, Y, X), None),
    ((ZH, X, ZL, Y), None),
    ((Y, ZH, ZL, X), None),
    ((ZH, ZL, Y, X), None),
    ((ZH, ZL, X, Y), None),
    ((ZH, X, Y, ZL), None),
)
SCATTER = {
    "D1": (X, ZL, Y, ZH),
    "G1": (Y, ZL, X, ZH),
    "T1": (ZL, X, Y, ZH),
    "G0": (Y, X, ZL, ZH),
    "T0": (X, Y, ZL, ZH),
}
ORDER = (
    "g40", "g10", "g20", "g00", "g50", "g01", "g30", "g21", "g11", "g02", "g31", "g51", "g12",
    "g32", "g52", "g03", "g33", "g13", "g53", "g22", "w1", "g41", "w0", "v0", "g23", "v3", "w3",
    "g42", "A0", "w2", "dg42", "v1", "g43", "xa0", "F0", "v2", "w4", "w5", "L0", "A1", "v5", "xf0",
    "xa1", "v4", "F1", "B1", "xf1", "dxa0", "K1", "xs1", "B0", "xt1", "G1", "rG10", "xs0", "D1",
    "G0", "rG00", "rG11", "L1", "T1", "rD10", "K0", "rG12", "rT10", "xt0", "rG01", "T0", "rD11",
    "rT00", "oa", "rT11", "rG02", "rD12", "doa", "rT01", "ob", "rG13", "rT12", "rG03", "oi", "rD13",
    "zG1", "rT02", "zG0", "rT13", "rT03", "zD1", "hG", "zT1", "zT0", "hT", "u1", "u2",
)

def order_masks(order):
    masks = [0]
    for bit in order:
        masks = masks + [m ^ bit for m in masks]
    return masks


def mirrored(order):
    return tuple({X: Y, Y: X}.get(bit, bit) for bit in order)


def flip(value, bit, count, other=None):
    if other is None or other == bit:
        return lax.ppermute(value, "dp", [(i, i ^ bit) for i in range(count)])
    pairs = [(i, i ^ bit) for i in range(count)]
    pairs += [(count + i, count + (i ^ other)) for i in range(count)]
    return lax.ppermute(value, ("section", "dp"), pairs)


def swap(value):
    return lax.ppermute(value, "section", [(0, 1), (1, 0)])


def rope_consts():
    position = np.arange(SLOT)
    index = np.maximum(position - 1, 0)
    started = (position > 0).astype(np.float32)
    row_pos = (index // WIDE).astype(np.float32) * started
    col_pos = (index % WIDE).astype(np.float32) * started
    quarter = HEAD_DIM // 4
    freq = np.power(np.float32(10000.0), -np.arange(quarter, dtype=np.float32) / quarter)
    row_angle = row_pos[:, None] * freq[None, :]
    col_angle = col_pos[:, None] * freq[None, :]
    angle = np.concatenate([row_angle, row_angle, col_angle, col_angle], axis=1)
    angle = np.concatenate([angle, angle], axis=1).astype(np.float32)
    even = (np.arange(LANES) // quarter) % 2 == 0
    sine = np.sin(angle)
    return (
        np.cos(angle).astype(np.float32),
        np.where(even, -sine, 0.0).astype(np.float32),
        np.where(even, 0.0, sine).astype(np.float32),
    )


def dot(left, right):
    return jnp.dot(left, right, preferred_element_type=F32)


def dot_nt(left, right):
    return lax.dot_general(left, right, (((1,), (1,)), ((), ())), preferred_element_type=F32)


def dot_tn(left, right):
    return lax.dot_general(left, right, (((0,), (0,)), ((), ())), preferred_element_type=F32)


def turn(value, sin_a, sin_b):
    return pltpu.roll(value, LANES - 16, 1) * sin_a + pltpu.roll(value, 16, 1) * sin_b


def params(steps=1):
    return pltpu.CompilerParams(
        dimension_semantics=("arbitrary",) * steps, vmem_limit_bytes=VMEM_BYTES
    )


def cost(flops, nbytes):
    return pl.CostEstimate(flops=1, bytes_accessed=1, transcendentals=0)


def shape(*dims, dtype=BF16):
    return jax.ShapeDtypeStruct(dims, dtype)


def kept(*dims, dtype=BF16):
    return pltpu.HBM(dims, dtype)


def far(*arrays):
    return tuple(pltpu.with_memory_space_constraint(a, pltpu.HBM) for a in arrays)


def launch(kernel, prefetch, grid, inputs, in_specs, out_shape, out_specs, work, scratch=()):
    return pl.pallas_call(
        kernel,
        grid_spec=pltpu.PrefetchScalarGridSpec(
            num_scalar_prefetch=len(prefetch),
            grid=grid,
            in_specs=list(in_specs),
            out_specs=out_specs,
            scratch_shapes=list(scratch),
        ),
        out_shape=out_shape,
        compiler_params=params(len(grid)),
        cost_estimate=work,
    )(*prefetch, *inputs)


def head_split(pair):
    lane = lax.broadcasted_iota(jnp.int32, pair.shape, 1)
    zero = jnp.zeros_like(pair)
    return jnp.where(lane < HEAD_DIM, pair, zero), jnp.where(lane < HEAD_DIM, zero, pair)


class Gathered:
    def __init__(self, sources, dims, masks=None, pieces=None):
        self.sources, self.dims, self.masks, self.pieces = tuple(sources), dims, masks, pieces

    def load(self, info, srcs, mats):
        if self.masks is None:
            for src, mat in zip(srcs, mats):
                mat[...] = src[...]
            return
        for section in range(2):

            @pl.when(info[1] == section)
            def _():
                for side in range(2):
                    part = section ^ side
                    for at, mask in enumerate(self.masks[part]):
                        src, shard = srcs[2 * side + at // 8], info[0] ^ mask
                        for row_from, rows, matrix, rest in self.pieces[part]:
                            mats[matrix][(shard, *rest)] = src[at % 8, row_from : row_from + rows]

    def scratch(self):
        kinds = [pltpu.VMEM(d, BF16) for d in self.dims]
        return kinds + [pltpu.SemaphoreType.DMA((len(self.dims),))]


def matrix(ref, rows=None, cols=slice(None)):
    if rows is not None:
        n, count = rows
        size = ref.shape[0] // count
        value = ref[pl.ds(pl.multiple_of(n * size, size), size)]
    else:
        value = ref[(slice(None),) * (len(ref.shape) - 1) + (cols,)]
    return value.reshape(-1, value.shape[-1])


ANYWHERE = pl.BlockSpec(memory_space=pl.ANY)


def loaded(gathered, kernel, n_in, n_out, info, *refs):
    n_src, n_mat = len(gathered.sources), len(gathered.dims)
    ins, srcs, refs = refs[:n_in], refs[n_in : n_in + n_src], refs[n_in + n_src :]
    outs, wholes, refs = refs[:n_out], refs[n_out : n_out + n_mat], refs[n_out + n_mat :]
    mats, out_sems, refs = refs[:n_mat], refs[n_mat], refs[n_mat + 1 :]
    step = pl.program_id(0)
    back = [
        pltpu.make_async_copy(mat, whole, out_sems.at[n])
        for n, (mat, whole) in enumerate(zip(mats, wholes))
    ]

    @pl.when(step == 0)
    def _():
        gathered.load(info, srcs, mats)
        for copy in back:
            copy.start()

    kernel(info, *ins, *mats, *outs, *refs)

    @pl.when(step == pl.num_programs(0) - 1)
    def _():
        for copy in back:
            copy.wait()


def launch_loaded(
    gathered, kernel, prefetch, grid, inputs, in_specs, out_shape, out_specs, work, scratch=()
):
    n_in = len(prefetch) - 1 + len(inputs)
    return launch(
        functools.partial(loaded, gathered, kernel, n_in, len(out_shape)),
        prefetch,
        grid,
        (*inputs, *gathered.sources),
        [*in_specs, *[pl.BlockSpec(memory_space=pltpu.VMEM)] * len(gathered.sources)],
        [*out_shape, *[kept(*d) for d in gathered.dims]],
        [*out_specs, *[ANYWHERE] * len(gathered.dims)],
        work,
        [*gathered.scratch(), *scratch],
    )


def attention_kernel(
    info, lim, x_ref, cos, sin_a, sin_b, wq, wk, wv, wo, act_ref, qkv_ref, probs_ref, scale_ref
):
    image = pl.program_id(0)
    x = x_ref[...].astype(F32)
    r = lax.rsqrt(jnp.mean(x * x, axis=1, keepdims=True) + EPS)
    normed = (x * r).astype(BF16)
    act_ref[:, :D] = normed
    scale_ref[...] = jnp.broadcast_to(r, (SLOT, LANES))
    for part, weight in enumerate((wq, wk)):
        full = dot(normed, matrix(weight))
        for p in range(PAIRS):
            piece = full[:, p * LANES : (p + 1) * LANES]
            piece = piece * cos[...] + turn(piece, sin_a[...], sin_b[...])
            start = part * D + p * LANES
            qkv_ref[:, start : start + LANES] = piece.astype(BF16)
    qkv_ref[:, 2 * D :] = dot(normed, matrix(wv)).astype(BF16)
    row = lax.broadcasted_iota(jnp.int32, (SLOT, SLOT), 0)
    col = lax.broadcasted_iota(jnp.int32, (SLOT, SLOT), 1)
    mask = (col <= row) & (col < lim[info[1] * 2 + image])
    for p in range(PAIRS):
        lanes = slice(p * LANES, (p + 1) * LANES)
        query = qkv_ref[:, lanes]
        keys = head_split(qkv_ref[:, D + p * LANES : D + (p + 1) * LANES])
        values = head_split(qkv_ref[:, 2 * D + p * LANES : 2 * D + (p + 1) * LANES])
        probs = []
        for h in range(2):
            scores = jnp.where(mask, dot_nt(query, keys[h]), -1e30)
            top = jnp.max(scores, axis=1, keepdims=True)
            raised = jnp.exp(scores - top)
            total = jnp.sum(raised, axis=1, keepdims=True)
            probs.append((raised * (1.0 / total)).astype(BF16))
            probs_ref[0, 2 * p + h] = probs[h]
        mixed = dot(jnp.concatenate(probs, axis=1), jnp.concatenate(values, axis=0))
        act_ref[:, D + p * LANES : D + (p + 1) * LANES] = mixed.astype(BF16)


def attention(info, lim, x, x_rows, gathered, tables):
    table = pl.BlockSpec((SLOT, LANES), lambda i, info, lim: (0, 0))
    return launch_loaded(
        gathered,
        attention_kernel,
        (info, lim),
        (2,),
        (x, *tables),
        [
            pl.BlockSpec((SLOT, D), lambda i, info, lim: (info[x_rows] * 2 + i, 0)),
            table,
            table,
            table,
        ],
        [
            shape(2 * SLOT, 2 * D),
            kept(2 * SLOT, 3 * D),
            kept(2, HEADS, SLOT, SLOT),
            kept(2 * SLOT, LANES, dtype=F32),
        ],
        [
            pl.BlockSpec((SLOT, 2 * D), lambda i, info, lim: (i, 0)),
            pl.BlockSpec((SLOT, 3 * D), lambda i, info, lim: (i, 0)),
            pl.BlockSpec((1, HEADS, SLOT, SLOT), lambda i, info, lim: (i, 0, 0, 0)),
            pl.BlockSpec((SLOT, LANES), lambda i, info, lim: (i, 0)),
        ],
        cost(3.6e9 + 24 * 4 * 256 * 256 * 128, 12e6),
    )


FBLOCK = 512


PACK = 1024


def feed_kernel(info, x_ref, mixed_ref, wo, wg, wu, middle_ref, scale_ref, pack_ref, s1_ref, s2_ref, normed):
    step = pl.program_id(0)
    lead = PACK // FBLOCK

    @pl.when(step == 0)
    def _():
        middle = x_ref[...].astype(F32) + dot(mixed_ref[...], wo[...])
        r = lax.rsqrt(jnp.mean(middle * middle, axis=1, keepdims=True) + EPS)
        middle_ref[...] = middle
        scale_ref[...] = jnp.broadcast_to(r, scale_ref.shape)
        normed[:, :D] = (middle * r).astype(BF16)
        normed[:, D:] = jnp.zeros((normed.shape[0], PACK - D), BF16)

    for part in range(lead):

        @pl.when(step == part)
        def _():
            pack_ref[...] = normed[:, part * FBLOCK : (part + 1) * FBLOCK]

    @pl.when(step >= lead)
    def _():
        cols = pl.ds(pl.multiple_of((step - lead) * FBLOCK, FBLOCK), FBLOCK)
        cols = slice(None) if wg.shape[-1] == FBLOCK else cols
        gate = dot(normed[:, :D], matrix(wg, cols=cols))
        up = dot(normed[:, :D], matrix(wu, cols=cols))
        sig = 0.5 * jnp.tanh(0.5 * gate) + 0.5
        silu = gate * sig
        pack_ref[...] = (silu * up).astype(BF16)
        s1_ref[...] = (up * (sig * (1.0 + gate * (1.0 - sig)))).astype(BF16)
        s2_ref[...] = silu.astype(BF16)


def feed(info, x, x_rows, act, wo, w):
    rows = 2 * SLOT
    lead = PACK // FBLOCK
    whole = lambda j, info: (0, 0)
    late = lambda j: jnp.maximum(j - lead, 0)
    wide = pl.BlockSpec((rows, FBLOCK), lambda j, info: (0, late(j)))
    args = (
        (info,),
        (lead + FF // FBLOCK,),
        (x, act, wo),
        [
            pl.BlockSpec((rows, D), lambda j, info: (info[x_rows], 0)),
            pl.BlockSpec((rows, D), lambda j, info: (0, 1)),
            pl.BlockSpec((D, D), whole),
        ],
        [
            shape(rows, D, dtype=F32),
            kept(rows, LANES, dtype=F32),
            shape(rows, PACK + FF),
            kept(rows, FF),
            kept(rows, FF),
        ],
        [
            pl.BlockSpec((rows, D), whole),
            pl.BlockSpec((rows, LANES), whole),
            pl.BlockSpec((rows, FBLOCK), lambda j, info: (0, j)),
            wide,
            wide,
        ],
        cost(2 * rows * D * (D + 2 * FF), 18e6),
        [pltpu.VMEM((rows, PACK), BF16)],
    )
    if isinstance(w, Gathered):
        return launch_loaded(w, feed_kernel, *args)
    prefetch, grid, inputs, in_specs, *rest = args
    gate = pl.BlockSpec((D, FBLOCK), lambda j, info: (0, late(j)))
    up = pl.BlockSpec((D, FBLOCK), lambda j, info: (1, late(j)))
    in_specs = [*in_specs, gate, up]
    return launch(feed_kernel, prefetch, grid, (*inputs, *far(w, w)), in_specs, *rest)


def leave_kernel(info, lim, middle_ref, low, high, wd, out_ref):
    image = pl.program_id(0)
    result = middle_ref[...] + dot(low[...], matrix(wd, (0, 2))) + dot(high[...], matrix(wd, (1, 2)))
    row = lax.broadcasted_iota(jnp.int32, result.shape, 0)
    out_ref[...] = jnp.where(row < lim[info[1] * 2 + image], result, 0.0).astype(BF16)


def leave(info, lim, middle, pack, wd):
    rows = 2 * SLOT
    args = (
        (info, lim),
        (2,),
        (middle, pack, pack),
        [
            pl.BlockSpec((SLOT, D), lambda i, info, lim: (i, 0)),
            pl.BlockSpec((SLOT, PACK), lambda i, info, lim: (i, 1)),
            pl.BlockSpec((SLOT, PACK), lambda i, info, lim: (i, 2)),
        ],
        [shape(rows, D)],
        [pl.BlockSpec((SLOT, D), lambda i, info, lim: (i, 0))],
        cost(2 * rows * D * FF, 8e6),
    )
    if isinstance(wd, Gathered):
        return launch_loaded(wd, leave_kernel, *args)
    prefetch, grid, inputs, in_specs, *rest = args
    in_specs = [*in_specs, pl.BlockSpec((FF, D), lambda i, info, lim: (0, 0))]
    return launch(leave_kernel, prefetch, grid, (*inputs, wd), in_specs, *rest)


GRADS = FF + FBLOCK


def feed_back_kernel(
    info,
    grad_ref,
    wg,
    wu,
    s1_ref,
    s2_ref,
    normed_ref,
    scale_ref,
    wo,
    wd,
    keep_ref,
    send_ref,
    gmid_ref,
    gmix_ref,
    total,
):
    step = pl.program_id(0)
    per_half = FHALF // FBLOCK
    down = wd[...] if wd.shape[0] == FBLOCK else matrix(wd, (step, FF // FBLOCK))
    grad_hidden = dot_nt(grad_ref[...], down)
    ggate = (grad_hidden * s1_ref[...].astype(F32)).astype(BF16)
    gup = (grad_hidden * s2_ref[...].astype(F32)).astype(BF16)
    at = pl.multiple_of((step % per_half) * FBLOCK, FBLOCK)
    own = (step // per_half) == info[1]

    @pl.when(own)
    def _():
        keep_ref[:, pl.ds(at, FBLOCK)] = ggate
        keep_ref[:, pl.ds(at + FHALF, FBLOCK)] = gup

    @pl.when(jnp.logical_not(own))
    def _():
        send_ref[:, pl.ds(at, FBLOCK)] = ggate
        send_ref[:, pl.ds(at + FHALF, FBLOCK)] = gup

    part = dot_nt(ggate, wg[...]) + dot_nt(gup, wu[...])

    @pl.when(step == 0)
    def _():
        total[...] = part

    @pl.when(step > 0)
    def _():
        total[...] += part

    @pl.when(step == pl.num_programs(0) - 1)
    def _():
        gn = total[...]
        normed = normed_ref[...].astype(F32)
        mean = jnp.mean(gn * normed, axis=1, keepdims=True)
        gmid = grad_ref[...].astype(F32) + scale_ref[:, :1] * (gn - normed * mean)
        gz = gmid.astype(BF16)
        gmid_ref[...] = gmid
        gmix_ref[...] = dot_nt(gz, wo[...]).astype(BF16)
        pad = jnp.zeros((gz.shape[0], GRADS - FF - HALF), BF16)
        for h in range(2):

            @pl.when(info[1] == h)
            def _():
                for out, half in ((keep_ref, h), (send_ref, 1 - h)):
                    out[:, FF : FF + HALF] = gz[:, half * HALF : (half + 1) * HALF]
                    out[:, FF + HALF :] = pad


def feed_back(info, grad, grad_rows, wd, wg, wu, up_row, s1, s2, pack, scale, wo):
    rows = 2 * SLOT
    whole = lambda j, info: (0, 0)
    col = pl.BlockSpec((D, FBLOCK), lambda j, info: (0, j))
    wide = pl.BlockSpec((rows, FBLOCK), lambda j, info: (0, j))
    full = pl.BlockSpec((rows, D), whole)
    args = (
        (info,),
        (FF // FBLOCK,),
        (grad, *far(wg, wu, s1, s2), pack, *far(scale, wo)),
        [
            pl.BlockSpec((rows, D), lambda j, info: (info[grad_rows], 0)),
            col,
            pl.BlockSpec((D, FBLOCK), lambda j, info: (up_row, j)),
            wide,
            wide,
            full,
            pl.BlockSpec((rows, LANES), whole),
            pl.BlockSpec((D, D), whole),
        ],
        [
            shape(rows, GRADS),
            shape(rows, GRADS),
            shape(rows, D, dtype=F32),
            shape(rows, D),
        ],
        [
            pl.BlockSpec((rows, GRADS), whole),
            pl.BlockSpec((rows, GRADS), whole),
            full,
            full,
        ],
        cost(2 * rows * D * (3 * FF + D), 24e6),
        [pltpu.VMEM((rows, D), F32)],
    )
    if isinstance(wd, Gathered):
        return launch_loaded(wd, feed_back_kernel, *args)
    prefetch, grid, inputs, in_specs, *rest = args
    in_specs = [*in_specs, pl.BlockSpec((FBLOCK, D), lambda j, info: (j, 0))]
    return launch(feed_back_kernel, prefetch, grid, (*inputs, *far(wd)), in_specs, *rest)


def attention_back_kernel(
    info,
    gmix_ref,
    qkv_ref,
    probs_ref,
    wq,
    wk,
    wv,
    normed_ref,
    scale_ref,
    gmid_ref,
    cos,
    sin_a,
    sin_b,
    gin_ref,
    keep_ref,
    send_ref,
    grads,
):
    for p in range(PAIRS):
        lanes = slice(p * LANES, (p + 1) * LANES)
        gmix = gmix_ref[:, lanes]
        query = head_split(qkv_ref[:, lanes])
        keys = head_split(qkv_ref[:, D + p * LANES : D + (p + 1) * LANES])
        values = head_split(qkv_ref[:, 2 * D + p * LANES : 2 * D + (p + 1) * LANES])
        gmix_parts = head_split(gmix)
        gs_parts = []
        for h in range(2):
            probs = probs_ref[0, 2 * p + h].astype(F32)
            weighted = probs * dot_nt(gmix, values[h])
            inner = jnp.sum(weighted, axis=1, keepdims=True)
            gs_parts.append((weighted - probs * inner).astype(BF16))
        gq = dot(jnp.concatenate(gs_parts, axis=1), jnp.concatenate(keys, axis=0))
        gk = dot_tn(gs_parts[0], query[0]) + dot_tn(gs_parts[1], query[1])
        gv = dot_tn(probs_ref[0, 2 * p], gmix_parts[0]) + dot_tn(
            probs_ref[0, 2 * p + 1], gmix_parts[1]
        )
        gq = gq * cos[...] - turn(gq, sin_a[...], sin_b[...])
        gk = gk * cos[...] - turn(gk, sin_a[...], sin_b[...])
        grads[0, :, lanes] = gq.astype(BF16)
        grads[1, :, lanes] = gk.astype(BF16)
        grads[2, :, lanes] = gv.astype(BF16)
    gn = dot_nt(grads[0], wq[...]) + dot_nt(grads[1], wk[...]) + dot_nt(grads[2], wv[...])
    normed = normed_ref[...].astype(F32)
    mean = jnp.mean(gn * normed, axis=1, keepdims=True)
    gin = gmid_ref[...] + scale_ref[:, :1] * (gn - normed * mean)
    gin_ref[...] = gin.astype(BF16)
    send_ref[:, 3 * HALF :] = gin.astype(BF16)
    for h in range(2):

        @pl.when(info[1] == h)
        def _():
            for out, half in ((keep_ref, h), (send_ref, 1 - h)):
                cols = slice(half * HALF, (half + 1) * HALF)
                for part in range(3):
                    out[:, part * HALF : (part + 1) * HALF] = grads[part, :, cols]


def attention_back(info, gmix, qkv, probs, wq, wk, wv, act, scale, gmid, tables):
    rows = 2 * SLOT
    whole = lambda i, info: (0, 0)
    table = pl.BlockSpec((SLOT, LANES), whole)
    weight = pl.BlockSpec((D, D), whole)
    full = pl.BlockSpec((SLOT, D), lambda i, info: (i, 0))
    pack = pl.BlockSpec((SLOT, 3 * HALF), lambda i, info: (i, 0))
    longer = pl.BlockSpec((SLOT, 5 * HALF), lambda i, info: (i, 0))
    return launch(
        attention_back_kernel,
        (info,),
        (2,),
        (gmix, *far(qkv, probs, wq, wk, wv), act, *far(scale), gmid, *tables),
        [
                full,
                pl.BlockSpec((SLOT, 3 * D), lambda i, info: (i, 0)),
                pl.BlockSpec((1, HEADS, SLOT, SLOT), lambda i, info: (i, 0, 0, 0)),
                weight,
                weight,
                weight,
                full,
                pl.BlockSpec((SLOT, LANES), lambda i, info: (i, 0)),
                full,
                table,
                table,
                table,
            ],
        [shape(rows, D), shape(rows, 3 * HALF), shape(rows, 5 * HALF)],
        [full, pack, longer],
        cost(2 * rows * D * 3 * D + 24 * 8 * 256 * 256 * 128, 16e6),
        [pltpu.VMEM((3, SLOT, D), BF16)],
    )


def spread(info, where, scratch, rows, lane_blocks, outs, row_to):
    for place in range(16):
        if len(outs) == 2:
            low, high = where[0][place], where[1][place]
            shard = info[0] ^ (low + (high - low) * info[1])
        else:
            shard = ((info[0] ^ where[place % 4]) & 12) + place // 4
        at = pl.multiple_of(shard * rows, 16)
        out = outs[place // 8] if len(outs) == 2 else outs[0]
        slot = place % 8 if len(outs) == 2 else place
        for block in range(lane_blocks):
            out[slot, pl.ds(row_to + block * rows, rows), :] = scratch[
                pl.ds(at, rows), block * LANES : (block + 1) * LANES
            ]


def spread_shapes(planar, rows):
    count, dims = (1, (16, rows, LANES)) if planar else (2, (8, rows, LANES))
    return [shape(*dims)] * count, [pl.BlockSpec(dims, lambda j, info: (0, 0, 0))] * count


def feed_weight_kernel(where, gates, downs, info, *refs):
    rows = 2 * SLOT
    steps = FF // FBLOCK
    first = (steps + 1) * gates
    outs = list(refs[: len(refs) - 2 * gates - downs])
    refs = list(refs[len(outs) :])
    if gates:
        (own_ref, oth_ref, act_own, act_oth, g_own, g_oth), outs = outs[:6], outs[6:]
        turned, tile = refs[:2]
    if downs:
        (hid_own, hid_oth, gf_own, gf_oth), outs = outs[:4], outs[4:]
        down = refs[-1]
    step = pl.program_id(0)
    if gates:

        @pl.when(step == 0)
        def _():
            turned[:, :rows] = own_ref[...].T
            turned[:, rows:] = oth_ref[...].T

        @pl.when(step == steps)
        def _():
            turned[:, :rows] = act_own[...].T
            turned[:, rows:] = act_oth[...].T

        @pl.when(step <= steps)
        def _():
            tile[...] = (
                dot(turned[:, :rows], g_own[...]) + dot(turned[:, rows:], g_oth[...])
            ).astype(BF16)

        @pl.when(step < steps)
        def _():
            spread(info, where, tile, 48, 4, outs, pl.multiple_of(step * 192, 16))

        @pl.when(step == steps)
        def _():
            spread(info, where, tile, 48, 3, outs, 768)

    if downs:

        @pl.when(step >= first)
        def _():
            at = pl.multiple_of((step - first) * FBLOCK, FBLOCK)
            down[pl.ds(at, FBLOCK), :] = (
                dot_tn(hid_own[...], gf_own[...]) + dot_tn(hid_oth[...], gf_oth[...])
            ).astype(BF16)

        @pl.when(step == first + steps - 1)
        def _():
            spread(info, where, down, 128, 3, outs, 912 * gates)


def feed_weight(info, where, planar, gates, downs):
    rows = 2 * SLOT
    steps = FF // FBLOCK
    first = (steps + 1) * bool(gates)
    whole = lambda j, info: (0, 0)
    inputs, specs, scratch = [], [], []
    if gates:
        full = pl.BlockSpec((rows, D), whole)
        mixed = pl.BlockSpec((rows, D), lambda j, info: (0, 1))
        grad = pl.BlockSpec((rows, FBLOCK), lambda j, info: (0, jnp.minimum(j, steps)))
        inputs += gates
        specs += [full, full, mixed, mixed, grad, grad]
        scratch += [pltpu.VMEM((D, 2 * rows), BF16), pltpu.VMEM((D, FBLOCK), BF16)]
    if downs:
        *arrays, own_at, oth_at, col = downs
        hid = pl.BlockSpec(
            (rows, FBLOCK), lambda j, info: (0, jnp.maximum(j - first, 0) + PACK // FBLOCK)
        )
        inputs += arrays
        specs += [
            hid,
            hid,
            pl.BlockSpec((rows, HALF), lambda j, info: (info[own_at], info[1])),
            pl.BlockSpec((rows, HALF), lambda j, info: (info[oth_at], col + info[1])),
        ]
        scratch += [pltpu.VMEM((FF, HALF), BF16)]
    out_shape, out_specs = spread_shapes(planar, 912 * bool(gates) + 384 * bool(downs))
    return launch(
        functools.partial(feed_weight_kernel, where, bool(gates), bool(downs)),
        (info,),
        (first + steps * bool(downs),),
        inputs,
        specs,
        out_shape,
        out_specs,
        cost(2 * rows * D * 3 * FF, 20e6),
        scratch,
    )


def attention_weight_kernel(where, info, own_ref, oth_ref, g_own, g_oth, *refs):
    outs, (turned, tile) = refs[:-2], refs[-2:]
    step = pl.program_id(0)
    rows = 2 * SLOT

    @pl.when(step == 0)
    def _():
        turned[:, :rows] = own_ref[...].T
        turned[:, rows:] = oth_ref[...].T

    tile[...] = (
        dot(turned[:, :rows], g_own[...]) + dot(turned[:, rows:], g_oth[...])
    ).astype(BF16)
    spread(info, where, tile, 48, 3, outs, pl.multiple_of(step * 144, 16))


def attention_weight(info, where, planar, own, oth, g_own, g_oth):
    rows = 2 * SLOT
    full = pl.BlockSpec((rows, D), lambda j, info: (0, 0))
    grad = pl.BlockSpec((rows, HALF), lambda j, info: (0, j))
    out_shape, out_specs = spread_shapes(planar, 432)
    return launch(
        functools.partial(attention_weight_kernel, where),
        (info,),
        (3,),
        (own, oth, g_own, g_oth),
        [full, full, grad, grad],
        out_shape,
        out_specs,
        cost(2 * rows * D * 3 * D, 14e6),
        [pltpu.VMEM((D, 2 * rows), BF16), pltpu.VMEM((D, HALF), BF16)],
    )


def gather_plain(section, shards):
    mine = [lax.all_gather(s, "dp", axis=0, tiled=True) for s in shards]
    theirs = [swap(m) for m in mine]
    low = tuple(jnp.where(section == 0, m, t) for m, t in zip(mine, theirs))
    high = tuple(jnp.where(section == 0, t, m) for m, t in zip(mine, theirs))
    return low, high


def unpack_kernel(plan, gained, info, *refs):
    n_src = 1 + max(p[0] for p in plan)
    n_gain = len(gained)
    srcs, refs = refs[: 2 * n_src], refs[2 * n_src :]
    gain, weights, outs = refs[0], refs[1 : 1 + n_gain], refs[1 + n_gain :]
    for section in range(2):

        @pl.when(info[1] == section)
        def _():
            total = jnp.zeros((gain.shape[0], 1), F32)
            for n, (src, row_from, rows, row_to, scale, has_gain, out) in enumerate(plan):
                for side in range(2):
                    piece = srcs[2 * src + (section ^ side)]
                    width = outs[out].shape[1] // 2
                    for block in range(width // LANES):
                        at = row_from + block * rows
                        value = piece[at : at + rows, :]
                        col = side * width + block * LANES
                        if has_gain:
                            weight = weights[gained.index(n)][:, col : col + LANES].astype(F32)
                            total += scale * jnp.sum(weight * value, axis=1, keepdims=True)
                            value = value * (gain[...] * scale)
                        outs[out][row_to : row_to + rows, col : col + LANES] = value
            outs[-1][...] = jnp.broadcast_to(total, outs[-1].shape)


def unpack_all(info, plan, sources, gain, weights, dims):
    gained = tuple(n for n, p in enumerate(plan) if p[5])
    flat = [piece for source in sources for piece in source]
    return launch(
        functools.partial(unpack_kernel, plan, gained),
        (info,),
        (1,),
        (*flat, gain, *weights,),
        [pl.BlockSpec(v.shape, lambda i, info: (0, 0)) for v in (*flat, gain, *weights)],
        [shape(*d, dtype=F32) for d in dims],
        [pl.BlockSpec(d, lambda i, info: (0, 0)) for d in dims],
        cost(0, 8 * sum(a * b for a, b in dims)),
        (),
    )


def on_device(
    tokens,
    heights,
    out_grad,
    w_query,
    w_key,
    w_value,
    w_out,
    w_gate,
    w_up,
    w_down,
    gain_attn,
    gain_ffn,
):
    section = lax.axis_index("section")
    me = lax.axis_index("dp")
    count = lax.axis_size("dp")
    halving = count == 16
    rows = 2 * SLOT
    info = jnp.stack([me, section, 1 - section, jnp.zeros_like(me)]).astype(jnp.int32)
    own_rows, oth_rows, no_rows = 1, 2, 3
    token = [info]
    lim = WIDE * heights + 1
    gain_one = gain_attn[0].astype(F32)[:, None]
    gain_two = gain_ffn[0].astype(F32)[:, None]
    fold = lambda w, g: (w[0].astype(F32) * g).astype(BF16)
    shards = (
        fold(w_query, gain_one * SCALE),
        fold(w_key, gain_one),
        fold(w_value, gain_one),
        w_out[0],
        fold(w_gate, gain_two),
        fold(w_up, gain_two),
        w_down[0],
    )
    half, row = shards[6].shape[0] // 2, shards[0].shape[0]
    tables = tuple(jnp.asarray(t) for t in rope_consts())
    slots = jnp.arange(SLOT)
    valid = (slots[None, :] < lim[:, None]).reshape(-1, 1)
    grad = jnp.where(valid, out_grad, jnp.zeros_like(out_grad))

    def tie(*arrays):
        out = lax.optimization_barrier((*arrays, token[0]))
        token[0] = out[-1]
        return out[:-1] if len(arrays) > 1 else out[0]

    env = {}
    have, parts = {}, {}
    pair = lambda a, b: ((0, row, a, ()), (row, row, b, ()))
    pieces = (
        (pair(0, 1), pair(2, 3)),
        (((0, row, 0, ()),), ((0, row, 1, ()),)),
        (((0, half, 0, (0,)),), ((0, half, 0, (1,)),)),
    )
    if halving:
        dims = (((count, row, D),) * 4, ((count, row, FF),) * 2, ((count, 2, half, D),))
    else:
        dims = (((D, D),) * 4, ((D, FF),) * 2, ((FF, D),))
    flat = lambda found: tuple(w.reshape(-1, w.shape[-1]) for w in found)
    wholes, weights = {}, {}
    if halving:
        groups = (
            (jnp.concatenate(shards[0:2], axis=0), jnp.concatenate(shards[2:4], axis=0)),
            (shards[4], shards[5]),
            (shards[6][:half], shards[6][half:]),
        )
        for n, (first, second) in enumerate(groups):
            mine = jnp.where(section == 0, first, second)
            theirs = swap(jnp.where(section == 0, second, first))
            have[n] = jnp.where(section == 0, mine, theirs)[None]
            have[n + 3] = jnp.where(section == 0, theirs, mine)[None]
    else:
        for layer, found in enumerate(gather_plain(section, shards)):
            for group, some in enumerate((found[:4], found[4:6], found[6:])):
                wholes[3 * layer + group] = Gathered(some, dims[group])

    def double(stream, stage):
        order, after = GATHER[stream]
        if stage:
            env["g", stream, stage - 1] = got = tie(env["g", stream, stage - 1])
            have[stream] = jnp.concatenate([have[stream], got], axis=0)
        elif after is not None:
            env[("g",) + after] = tie(env[("g",) + after])
        have[stream] = tie(have[stream])
        env["g", stream, stage] = flip(
            have[stream], order[stage], count, mirrored(order)[stage]
        )

    def gathered(stream):
        if not halving:
            return wholes[stream]
        if ("q", stream) in env:
            return tie(env["q", stream])
        order = GATHER[stream][0]
        masks = (order_masks(order), order_masks(mirrored(order)))
        theirs, last = tie(env["w", stream], env["v", stream])
        sources = (have[stream], env["g", stream, 3], theirs, last)
        return Gathered(sources, dims[stream % 3], masks, pieces[stream % 3])

    plane = [[4 * z + i for i in range(4)] for z in range(4)]

    def reduce(name):
        env["c", name] = lax.psum_scatter(
            tie(env[name][0]), "dp", scatter_dimension=0, axis_index_groups=plane, tiled=True
        )

    def halve(name, stage):
        order = SCATTER[name]
        if stage:
            parts[name].append(tie(env["r", name, stage - 1]))
        elif len(order) == 2:
            parts[name] = [tie(env["c", name])]
        else:
            parts[name] = [env[name][0]]
        if stage == 0 and len(order) == 4:
            send = env[name][1]
        else:
            size = 1 << (len(order) - stage)
            send = sum(p[size // 2 : size].astype(F32) for p in parts[name]).astype(BF16)
        env["r", name, stage] = flip(tie(send), order[stage], count, mirrored(order)[stage])

    def total(name):
        parts[name].append(tie(env["r", name, len(SCATTER[name]) - 1]))
        env["z", name] = tie(sum(p[0].astype(F32) for p in parts[name]))

    def attend(layer):
        x, x_rows = (tokens, own_rows) if layer == 0 else (env["L", 0], no_rows)
        out = tie(*attention(token[0], lim, x, x_rows, gathered(3 * layer), tables))
        env["A", layer], weights[3 * layer] = out[:4], flat(out[4:])

    def feed_on(layer):
        x, x_rows = (tokens, own_rows) if layer == 0 else (env["L", 0], no_rows)
        w_o, source = weights[3 * layer][3], gathered(3 * layer + 1)
        out = tie(*feed(token[0], x, x_rows, env["A", layer][0], w_o, source))
        env["F", layer] = out[:5]
        weights[3 * layer + 1] = flat(out[5:]) if len(out) > 5 else (source, source)

    def leave_off(layer):
        middle, _, pack, _, _ = env["F", layer]
        w_d = gathered(2) if layer == 0 else weights[5][0]
        out = leave(token[0], lim, middle, pack, w_d)
        out = tie(*out) if len(out) > 1 else (tie(*out),)
        env["L", layer] = out[0]
        if layer == 0:
            weights[2] = flat(out[1:])

    def cotangent(layer):
        if layer == 1:
            return grad, grad, own_rows, oth_rows
        return env["K", 1][0], env.get("xt1"), no_rows, no_rows

    def feed_in(layer):
        own, _, at, _ = cotangent(layer)
        _, scale, pack, s1, s2 = env["F", layer]
        w_g, w_u = weights[3 * layer + 1]
        w_d = gathered(5) if layer == 1 else weights[2][0]
        w_o = weights[3 * layer][3]
        up_row = w_g.shape[0] // D - 1
        out = tie(*feed_back(token[0], own, at, w_d, w_g, w_u, up_row, s1, s2, pack, scale, w_o))
        env["B", layer] = out[:4]
        if layer == 1:
            weights[5] = flat(out[4:])

    def attend_in(layer):
        act, qkv, probs, scale = env["A", layer]
        _, _, gmid, gmix = env["B", layer]
        w = weights[3 * layer][:3]
        env["K", layer] = tie(
            *attention_back(token[0], gmix, qkv, probs, *w, act, scale, gmid, tables)
        )

    def form(name):
        layer = int(name[1])
        order = SCATTER[name][::-1]
        planar = len(order) == 2
        where = order_masks(order) if planar else (order_masks(order), order_masks(mirrored(order)))
        if name[0] in "DG":
            key = "xf%d" % layer
            pack, env[key] = env["F", layer][2], tie(env[key])
            gates, downs = (), ()
            if name[0] == "G":
                more = "xa%d" % layer
                env[more], recv = tie(env[more], env["xs%d" % layer])
                act, keep = env["A", layer][0], env["B", layer][0]
                gates = (pack, env[key], act, env[more], keep, recv)
            if name[0] == "D" or "D%d" % layer not in SCATTER:
                if layer == 0:
                    env["xt1"] = tie(env["xt1"])
                own, oth, at, oth_at = cotangent(layer)
                downs = (pack, env[key], own, oth, at, oth_at, 0 if layer == 1 else 3)
            made = feed_weight(token[0], where, planar, gates, downs)
        else:
            more = "xa%d" % layer
            env[more], recv = tie(env[more], env["xt%d" % layer])
            other = env[more]
            args = (env["A", layer][0], other, env["K", layer][1], recv)
            made = attention_weight(token[0], where, planar, *args)
        env[name] = tie(*made) if len(made) > 1 else (tie(*made),)

    sent = {
        "a": lambda layer: env["A", layer][0],
        "f": lambda layer: env["F", layer][2],
        "s": lambda layer: env["B", layer][1],
        "t": lambda layer: env["K", layer][2],
    }

    def both(mine, theirs):
        low = jnp.concatenate([mine, theirs], axis=0)
        return jnp.where(section == 0, low, jnp.concatenate([theirs, mine], axis=0))[None]

    pick = lambda first, second: jnp.where(section == 0, first, second)

    def unpacked(names, plan, gain, local, out_dims):
        sources = [(env["m", n], tie(env["h", n])) for n in names]
        return unpack_all(token[0], plan, sources, gain, local, out_dims)

    def run(name):
        kind, rest = name[0], name[1:]
        if kind == "g":
            double(int(rest[0]), int(rest[1]))
        elif kind == "w":
            env["w", int(rest)] = swap(tie(have[int(rest)]))
        elif kind == "v":
            key = ("g", int(rest), 3)
            env[key] = tie(env[key])
            env["v", int(rest)] = swap(env[key])
        elif kind == "q":
            stream = int(rest)
            part = tie(have[stream])[0]
            env["q", stream] = lax.all_gather(part, ("section", "dp"), tiled=True)
        elif kind == "c":
            reduce(rest)
        elif kind == "r":
            halve(rest[:2], int(rest[2]))
        elif kind == "z":
            total(rest)
        elif kind == "d":
            kind, rest = rest[0], rest[1:]
            keys = {
                "g": lambda: ("g", int(rest[0]), int(rest[1])),
                "r": lambda: ("r", rest[:2], int(rest[2])),
                "x": lambda: "x" + rest,
                "o": lambda: "o" + rest,
                "h": lambda: ("h", rest),
                "c": lambda: ("c", rest),
            }
            key = keys.get(kind, lambda: (kind, int(rest)))()
            env[key] = tie(env[key])
        elif kind == "x":
            env[name] = swap(tie(sent[rest[0]](int(rest[1]))))
        elif kind == "h":
            first, second = (
                jnp.concatenate([env["z", k + at] for k in rest + "D" if ("z", k + at) in env])
                if rest == "G"
                else env["z", rest + at]
                for at in "01"
            )
            env["m", rest], other = tie(pick(first, second), pick(second, first))
            env["h", rest] = swap(other)
        elif name == "u1":
            side = row * FHALF // LANES
            last = 2 * side + row * HALF // LANES
            plan = (
                (0, 0, row, 0, 1.0, True, 0),
                (0, side, row, 0, 1.0, True, 1),
                (0, 2 * side, row, 0, 1.0, False, 2),
                (0, last, 2 * half, 0, 1.0, False, 3),
            )
            out_dims = ((row, FF), (row, FF), (row, D), (2 * half, D), (row, LANES))
            env["u1"] = unpacked("G", plan, gain_two, (w_gate[0], w_up[0]), out_dims)
        elif name == "u2":
            side = row * HALF // LANES
            plan = (
                (0, 0, row, 0, SCALE, True, 0),
                (0, side, row, 0, 1.0, True, 1),
                (0, 2 * side, row, 0, 1.0, True, 2),
            )
            local = (w_query[0], w_key[0], w_value[0])
            out_dims = ((row, D),) * 3 + ((row, LANES),)
            env["u2"] = unpacked("T", plan, gain_one, local, out_dims)
        elif name == "oa":
            env["oa"] = swap(tie(pick(env["L", 1], env["L", 0])))
        elif name == "ob":
            env["ob"] = both(pick(env["L", 0], env["L", 1]), tie(env["oa"]))
        elif name == "oi":
            other = [v[:, 3 * HALF :] for v in tie(env["xt0"], env["xt1"])]
            env["oi"] = both(pick(env["K", 0][0], env["K", 1][0]), pick(*other))
        else:
            layer = int(rest)
            {"A": attend, "F": feed_on, "L": leave_off, "B": feed_in, "K": attend_in}[kind](layer)

    for name in ORDER:
        if name[0] in "DGT":
            if halving:
                form(name)
        elif halving or name[0] in "xoAFLBK":
            run(name)

    if halving:
        grad_g, grad_u, grad_o, grad_d, gain_grad_two = env["u1"]
        grad_q, grad_k, grad_v, gain_grad_one = env["u2"]
        gain_grad_one, gain_grad_two = gain_grad_one[:, 0], gain_grad_two[:, 0]
    else:
        cut = lambda v, at: lax.dynamic_slice_in_dim(v, info[at] * rows, rows, 0)
        join = lambda a, b: jnp.concatenate([a, b], axis=0)

        def reduced(a, g):
            full = lax.dot_general(a, g, (((0,), (0,)), ((), ())), preferred_element_type=F32)
            return lax.psum_scatter(full, "dp", scatter_dimension=0, tiled=True)

        found = []
        for layer in range(2):
            own, oth, at, oth_at = cotangent(layer)
            oth = oth if layer == 1 else oth[:, 3 * HALF :]
            gf = lax.dynamic_slice_in_dim(
                join(cut(own, at), cut(oth, oth_at)), section * HALF, HALF, 1
            )
            acts = join(env["A", layer][0], env["xa%d" % layer])
            gts = join(env["K", layer][1], env["xt%d" % layer][:, : 3 * HALF])
            gus = join(env["B", layer][0], env["xs%d" % layer])
            pack = join(env["F", layer][2], env["xf%d" % layer])
            nor, hid = pack[:, :D], pack[:, PACK:]
            found.append(
                (
                    reduced(acts[:, :D], gts[:, :HALF]),
                    reduced(acts[:, :D], gts[:, HALF : 2 * HALF]),
                    reduced(acts[:, :D], gts[:, 2 * HALF :]),
                    reduced(acts[:, D:], gus[:, FF : FF + HALF]),
                    reduced(nor, gus[:, :FHALF]),
                    reduced(nor, gus[:, FHALF:FF]),
                    reduced(hid, gf),
                )
            )

        def cols(first, second):
            mine, theirs = pick(first, second), swap(pick(second, first))
            low = jnp.concatenate([mine, theirs], axis=1)
            return pick(low, jnp.concatenate([theirs, mine], axis=1))

        grads = [cols(first, second) for first, second in zip(*found)]
        grad_q, grad_k, grad_v, grad_o, grad_g, grad_u, grad_d = grads
        along = lambda w, g: jnp.sum(w[0].astype(F32) * g, axis=1)
        gain_grad_one = SCALE * along(w_query, grad_q)
        gain_grad_one += along(w_key, grad_k) + along(w_value, grad_v)
        gain_grad_two = along(w_gate, grad_g) + along(w_up, grad_u)
        grad_q, grad_k, grad_v = grad_q * (gain_one * SCALE), grad_k * gain_one, grad_v * gain_one
        grad_g, grad_u = grad_g * gain_two, grad_u * gain_two

    return (
        env["ob"],
        env["oi"],
        grad_q[None],
        grad_k[None],
        grad_v[None],
        grad_o[None],
        grad_g[None],
        grad_u[None],
        grad_d[None],
        gain_grad_one[None],
        gain_grad_two[None],
    )


def solution(mesh):
    rows = P("dp", None)
    weight = P("section", "dp", None)
    gain = P("section", "dp")
    return jax.shard_map(
        on_device,
        mesh=mesh,
        in_specs=(rows, P("dp"), rows) + (weight,) * 7 + (gain,) * 2,
        out_specs=(weight,) * 9 + (gain,) * 2,
        check_vma=False,
    )
```

```python
import functools

import jax
import jax.numpy as jnp
import numpy as np
from jax import lax
from jax.experimental import pallas as pl
from jax.experimental.pallas import tpu as pltpu
from jax.sharding import PartitionSpec as P

D = 768
HEADS = 12
HEAD_DIM = 64
FF = 2048
WIDE = 16
SLOT = 256
HALF = D // 2
FHALF = FF // 2
PAIRS = HEADS // 2
LANES = 128
EPS = 1e-05
SCALE = 0.125
F32 = jnp.float32
BF16 = jnp.bfloat16
VMEM_BYTES = 24 * 1024 * 1024

X, Y, ZL, ZH = 1, 2, 4, 8
GATHER = (
    ((ZH, ZL, Y, X), None),
    ((ZH, X, ZL, Y), None),
    ((Y, ZH, ZL, X), None),
    ((ZH, ZL, Y, X), None),
    ((ZH, ZL, Y, X), None),
    ((ZH, X, Y, ZL), None),
)
SCATTER = {
    "D1": (X, ZL, Y, ZH),
    "G1": (Y, ZL, X, ZH),
    "T1": (ZL, X, Y, ZH),
    "G0": (Y, X, ZL, ZH),
    "T0": (X, Y, ZL, ZH),
}
ORDER = (
    "g40", "g10", "g20", "g50", "g00", "g01", "g30", "g21", "g11", "dg30", "g31", "g02", "g51",
    "g12", "g32", "g52", "g03", "g33", "g53", "g13", "g22", "w1", "g41", "w0", "v0", "g23", "v3",
    "w3", "g42", "A0", "w2", "dg42", "v1", "g43", "xa0", "F0", "v2", "w4", "w5", "L0", "A1", "v5",
    "xf0", "xa1", "v4", "F1", "B1", "xf1", "dxa0", "K1", "xs1", "B0", "xt1", "G1", "rG10", "xs0",
    "D1", "G0", "rG00", "rG11", "L1", "T1", "rD10", "K0", "rG12", "rT10", "xt0", "rG01", "T0",
    "rD11", "rT00", "oa", "rT11", "rG02", "rD12", "doa", "rT01", "ob", "rG13", "rT12", "rG03",
    "rD13", "zG1", "rT02", "zG0", "rT13", "rT03", "zD1", "hG", "oi", "zT1", "zT0", "hT", "u1", "u2",
)

def order_masks(order):
    masks = [0]
    for bit in order:
        masks = masks + [m ^ bit for m in masks]
    return masks


def mirrored(order):
    return tuple({X: Y, Y: X}.get(bit, bit) for bit in order)


def flip(value, bit, count, other=None):
    if other is None or other == bit:
        return lax.ppermute(value, "dp", [(i, i ^ bit) for i in range(count)])
    pairs = [(i, i ^ bit) for i in range(count)]
    pairs += [(count + i, count + (i ^ other)) for i in range(count)]
    return lax.ppermute(value, ("section", "dp"), pairs)


def swap(value):
    return lax.ppermute(value, "section", [(0, 1), (1, 0)])


def rope_consts():
    position = np.arange(SLOT)
    index = np.maximum(position - 1, 0)
    started = (position > 0).astype(np.float32)
    row_pos = (index // WIDE).astype(np.float32) * started
    col_pos = (index % WIDE).astype(np.float32) * started
    quarter = HEAD_DIM // 4
    freq = np.power(np.float32(10000.0), -np.arange(quarter, dtype=np.float32) / quarter)
    row_angle = row_pos[:, None] * freq[None, :]
    col_angle = col_pos[:, None] * freq[None, :]
    angle = np.concatenate([row_angle, row_angle, col_angle, col_angle], axis=1)
    angle = np.concatenate([angle, angle], axis=1).astype(np.float32)
    even = (np.arange(LANES) // quarter) % 2 == 0
    sine = np.sin(angle)
    return (
        np.cos(angle).astype(np.float32),
        np.where(even, -sine, 0.0).astype(np.float32),
        np.where(even, 0.0, sine).astype(np.float32),
    )


def dot(left, right):
    return jnp.dot(left, right, preferred_element_type=F32)


def dot_nt(left, right):
    return lax.dot_general(left, right, (((1,), (1,)), ((), ())), preferred_element_type=F32)


def dot_tn(left, right):
    return lax.dot_general(left, right, (((0,), (0,)), ((), ())), preferred_element_type=F32)


def turn(value, sin_a, sin_b):
    return pltpu.roll(value, LANES - 16, 1) * sin_a + pltpu.roll(value, 16, 1) * sin_b


def params(steps=1):
    return pltpu.CompilerParams(
        dimension_semantics=("arbitrary",) * steps, vmem_limit_bytes=VMEM_BYTES
    )


def cost(flops, nbytes):
    return pl.CostEstimate(flops=1, bytes_accessed=1, transcendentals=0)


def shape(*dims, dtype=BF16):
    return jax.ShapeDtypeStruct(dims, dtype)


def kept(*dims, dtype=BF16):
    return pltpu.HBM(dims, dtype)


def far(*arrays):
    return tuple(pltpu.with_memory_space_constraint(a, pltpu.HBM) for a in arrays)


def launch(kernel, prefetch, grid, inputs, in_specs, out_shape, out_specs, work, scratch=()):
    return pl.pallas_call(
        kernel,
        grid_spec=pltpu.PrefetchScalarGridSpec(
            num_scalar_prefetch=len(prefetch),
            grid=grid,
            in_specs=list(in_specs),
            out_specs=out_specs,
            scratch_shapes=list(scratch),
        ),
        out_shape=out_shape,
        compiler_params=params(len(grid)),
        cost_estimate=work,
    )(*prefetch, *inputs)


def head_split(pair):
    lane = lax.broadcasted_iota(jnp.int32, pair.shape, 1)
    zero = jnp.zeros_like(pair)
    return jnp.where(lane < HEAD_DIM, pair, zero), jnp.where(lane < HEAD_DIM, zero, pair)


class Gathered:
    def __init__(self, sources, dims, masks=None, pieces=None):
        self.sources, self.dims, self.masks, self.pieces = tuple(sources), dims, masks, pieces

    def load(self, info, srcs, mats):
        if self.masks is None:
            for src, mat in zip(srcs, mats):
                mat[...] = src[...]
            return
        for section in range(2):

            @pl.when(info[1] == section)
            def _():
                for side in range(2):
                    part = section ^ side
                    for at, mask in enumerate(self.masks[part]):
                        src, shard = srcs[2 * side + at // 8], info[0] ^ mask
                        for row_from, rows, matrix, rest in self.pieces[part]:
                            mats[matrix][(shard, *rest)] = src[at % 8, row_from : row_from + rows]

    def scratch(self):
        kinds = [pltpu.VMEM(d, BF16) for d in self.dims]
        return kinds + [pltpu.SemaphoreType.DMA((len(self.dims),))]


def matrix(ref, rows=None, cols=slice(None)):
    if rows is not None:
        n, count = rows
        size = ref.shape[0] // count
        value = ref[pl.ds(pl.multiple_of(n * size, size), size)]
    else:
        value = ref[(slice(None),) * (len(ref.shape) - 1) + (cols,)]
    return value.reshape(-1, value.shape[-1])


ANYWHERE = pl.BlockSpec(memory_space=pl.ANY)


def loaded(gathered, kernel, n_in, n_out, info, *refs):
    n_src, n_mat = len(gathered.sources), len(gathered.dims)
    ins, srcs, refs = refs[:n_in], refs[n_in : n_in + n_src], refs[n_in + n_src :]
    outs, wholes, refs = refs[:n_out], refs[n_out : n_out + n_mat], refs[n_out + n_mat :]
    mats, out_sems, refs = refs[:n_mat], refs[n_mat], refs[n_mat + 1 :]
    step = pl.program_id(0)
    back = [
        pltpu.make_async_copy(mat, whole, out_sems.at[n])
        for n, (mat, whole) in enumerate(zip(mats, wholes))
    ]

    @pl.when(step == 0)
    def _():
        gathered.load(info, srcs, mats)
        for copy in back:
            copy.start()

    kernel(info, *ins, *mats, *outs, *refs)

    @pl.when(step == pl.num_programs(0) - 1)
    def _():
        for copy in back:
            copy.wait()


def launch_loaded(
    gathered, kernel, prefetch, grid, inputs, in_specs, out_shape, out_specs, work, scratch=()
):
    n_in = len(prefetch) - 1 + len(inputs)
    return launch(
        functools.partial(loaded, gathered, kernel, n_in, len(out_shape)),
        prefetch,
        grid,
        (*inputs, *gathered.sources),
        [*in_specs, *[pl.BlockSpec(memory_space=pltpu.VMEM)] * len(gathered.sources)],
        [*out_shape, *[kept(*d) for d in gathered.dims]],
        [*out_specs, *[ANYWHERE] * len(gathered.dims)],
        work,
        [*gathered.scratch(), *scratch],
    )


def attention_kernel(
    info, lim, x_ref, cos, sin_a, sin_b, wq, wk, wv, wo, act_ref, qkv_ref, probs_ref, scale_ref
):
    image = pl.program_id(0)
    x = x_ref[...].astype(F32)
    r = lax.rsqrt(jnp.mean(x * x, axis=1, keepdims=True) + EPS)
    normed = (x * r).astype(BF16)
    act_ref[:, :D] = normed
    scale_ref[...] = jnp.broadcast_to(r, (SLOT, LANES))
    for part, weight in enumerate((wq, wk)):
        full = dot(normed, matrix(weight))
        for p in range(PAIRS):
            piece = full[:, p * LANES : (p + 1) * LANES]
            piece = piece * cos[...] + turn(piece, sin_a[...], sin_b[...])
            start = part * D + p * LANES
            qkv_ref[:, start : start + LANES] = piece.astype(BF16)
    qkv_ref[:, 2 * D :] = dot(normed, matrix(wv)).astype(BF16)
    row = lax.broadcasted_iota(jnp.int32, (SLOT, SLOT), 0)
    col = lax.broadcasted_iota(jnp.int32, (SLOT, SLOT), 1)
    mask = (col <= row) & (col < lim[info[1] * 2 + image])
    for p in range(PAIRS):
        lanes = slice(p * LANES, (p + 1) * LANES)
        query = qkv_ref[:, lanes]
        keys = head_split(qkv_ref[:, D + p * LANES : D + (p + 1) * LANES])
        values = head_split(qkv_ref[:, 2 * D + p * LANES : 2 * D + (p + 1) * LANES])
        probs = []
        for h in range(2):
            scores = jnp.where(mask, dot_nt(query, keys[h]), -1e30)
            top = jnp.max(scores, axis=1, keepdims=True)
            raised = jnp.exp(scores - top)
            total = jnp.sum(raised, axis=1, keepdims=True)
            probs.append((raised * (1.0 / total)).astype(BF16))
            probs_ref[0, 2 * p + h] = probs[h]
        mixed = dot(jnp.concatenate(probs, axis=1), jnp.concatenate(values, axis=0))
        act_ref[:, D + p * LANES : D + (p + 1) * LANES] = mixed.astype(BF16)


def attention(info, lim, x, x_rows, gathered, tables):
    table = pl.BlockSpec((SLOT, LANES), lambda i, info, lim: (0, 0))
    return launch_loaded(
        gathered,
        attention_kernel,
        (info, lim),
        (2,),
        (x, *tables),
        [
            pl.BlockSpec((SLOT, D), lambda i, info, lim: (info[x_rows] * 2 + i, 0)),
            table,
            table,
            table,
        ],
        [
            shape(2 * SLOT, 2 * D),
            kept(2 * SLOT, 3 * D),
            kept(2, HEADS, SLOT, SLOT),
            kept(2 * SLOT, LANES, dtype=F32),
        ],
        [
            pl.BlockSpec((SLOT, 2 * D), lambda i, info, lim: (i, 0)),
            pl.BlockSpec((SLOT, 3 * D), lambda i, info, lim: (i, 0)),
            pl.BlockSpec((1, HEADS, SLOT, SLOT), lambda i, info, lim: (i, 0, 0, 0)),
            pl.BlockSpec((SLOT, LANES), lambda i, info, lim: (i, 0)),
        ],
        cost(3.6e9 + 24 * 4 * 256 * 256 * 128, 12e6),
    )


FBLOCK = 512


PACK = 1024


def feed_kernel(info, x_ref, mixed_ref, wo, wg, wu, middle_ref, scale_ref, pack_ref, s1_ref, s2_ref, normed):
    step = pl.program_id(0)
    lead = PACK // FBLOCK

    @pl.when(step == 0)
    def _():
        middle = x_ref[...].astype(F32) + dot(mixed_ref[...], wo[...])
        r = lax.rsqrt(jnp.mean(middle * middle, axis=1, keepdims=True) + EPS)
        middle_ref[...] = middle
        scale_ref[...] = jnp.broadcast_to(r, scale_ref.shape)
        normed[:, :D] = (middle * r).astype(BF16)
        normed[:, D:] = jnp.zeros((normed.shape[0], PACK - D), BF16)

    for part in range(lead):

        @pl.when(step == part)
        def _():
            pack_ref[...] = normed[:, part * FBLOCK : (part + 1) * FBLOCK]

    @pl.when(step >= lead)
    def _():
        cols = pl.ds(pl.multiple_of((step - lead) * FBLOCK, FBLOCK), FBLOCK)
        cols = slice(None) if wg.shape[-1] == FBLOCK else cols
        gate = dot(normed[:, :D], matrix(wg, cols=cols))
        up = dot(normed[:, :D], matrix(wu, cols=cols))
        sig = 0.5 * jnp.tanh(0.5 * gate) + 0.5
        silu = gate * sig
        pack_ref[...] = (silu * up).astype(BF16)
        s1_ref[...] = (up * (sig * (1.0 + gate * (1.0 - sig)))).astype(BF16)
        s2_ref[...] = silu.astype(BF16)


def feed(info, x, x_rows, act, wo, w):
    rows = 2 * SLOT
    lead = PACK // FBLOCK
    whole = lambda j, info: (0, 0)
    late = lambda j: jnp.maximum(j - lead, 0)
    wide = pl.BlockSpec((rows, FBLOCK), lambda j, info: (0, late(j)))
    args = (
        (info,),
        (lead + FF // FBLOCK,),
        (x, act, wo),
        [
            pl.BlockSpec((rows, D), lambda j, info: (info[x_rows], 0)),
            pl.BlockSpec((rows, D), lambda j, info: (0, 1)),
            pl.BlockSpec((D, D), whole),
        ],
        [
            shape(rows, D, dtype=F32),
            kept(rows, LANES, dtype=F32),
            shape(rows, PACK + FF),
            kept(rows, FF),
            kept(rows, FF),
        ],
        [
            pl.BlockSpec((rows, D), whole),
            pl.BlockSpec((rows, LANES), whole),
            pl.BlockSpec((rows, FBLOCK), lambda j, info: (0, j)),
            wide,
            wide,
        ],
        cost(2 * rows * D * (D + 2 * FF), 18e6),
        [pltpu.VMEM((rows, PACK), BF16)],
    )
    if isinstance(w, Gathered):
        return launch_loaded(w, feed_kernel, *args)
    prefetch, grid, inputs, in_specs, *rest = args
    gate = pl.BlockSpec((D, FBLOCK), lambda j, info: (0, late(j)))
    up = pl.BlockSpec((D, FBLOCK), lambda j, info: (1, late(j)))
    in_specs = [*in_specs, gate, up]
    return launch(feed_kernel, prefetch, grid, (*inputs, *far(w, w)), in_specs, *rest)


def leave_kernel(info, lim, middle_ref, low, high, wd, out_ref):
    image = pl.program_id(0)
    result = middle_ref[...] + dot(low[...], matrix(wd, (0, 2))) + dot(high[...], matrix(wd, (1, 2)))
    row = lax.broadcasted_iota(jnp.int32, result.shape, 0)
    out_ref[...] = jnp.where(row < lim[info[1] * 2 + image], result, 0.0).astype(BF16)


def leave(info, lim, middle, pack, wd):
    rows = 2 * SLOT
    args = (
        (info, lim),
        (2,),
        (middle, pack, pack),
        [
            pl.BlockSpec((SLOT, D), lambda i, info, lim: (i, 0)),
            pl.BlockSpec((SLOT, PACK), lambda i, info, lim: (i, 1)),
            pl.BlockSpec((SLOT, PACK), lambda i, info, lim: (i, 2)),
        ],
        [shape(rows, D)],
        [pl.BlockSpec((SLOT, D), lambda i, info, lim: (i, 0))],
        cost(2 * rows * D * FF, 8e6),
    )
    if isinstance(wd, Gathered):
        return launch_loaded(wd, leave_kernel, *args)
    prefetch, grid, inputs, in_specs, *rest = args
    in_specs = [*in_specs, pl.BlockSpec((FF, D), lambda i, info, lim: (0, 0))]
    return launch(leave_kernel, prefetch, grid, (*inputs, wd), in_specs, *rest)


GRADS = FF + FBLOCK


def feed_back_kernel(
    info,
    grad_ref,
    wg,
    wu,
    s1_ref,
    s2_ref,
    normed_ref,
    scale_ref,
    wo,
    wd,
    keep_ref,
    send_ref,
    gmid_ref,
    gmix_ref,
    total,
):
    step = pl.program_id(0)
    per_half = FHALF // FBLOCK
    down = wd[...] if wd.shape[0] == FBLOCK else matrix(wd, (step, FF // FBLOCK))
    grad_hidden = dot_nt(grad_ref[...], down)
    ggate = (grad_hidden * s1_ref[...].astype(F32)).astype(BF16)
    gup = (grad_hidden * s2_ref[...].astype(F32)).astype(BF16)
    at = pl.multiple_of((step % per_half) * FBLOCK, FBLOCK)
    own = (step // per_half) == info[1]

    @pl.when(own)
    def _():
        keep_ref[:, pl.ds(at, FBLOCK)] = ggate
        keep_ref[:, pl.ds(at + FHALF, FBLOCK)] = gup

    @pl.when(jnp.logical_not(own))
    def _():
        send_ref[:, pl.ds(at, FBLOCK)] = ggate
        send_ref[:, pl.ds(at + FHALF, FBLOCK)] = gup

    part = dot_nt(ggate, wg[...]) + dot_nt(gup, wu[...])

    @pl.when(step == 0)
    def _():
        total[...] = part

    @pl.when(step > 0)
    def _():
        total[...] += part

    @pl.when(step == pl.num_programs(0) - 1)
    def _():
        gn = total[...]
        normed = normed_ref[...].astype(F32)
        mean = jnp.mean(gn * normed, axis=1, keepdims=True)
        gmid = grad_ref[...].astype(F32) + scale_ref[:, :1] * (gn - normed * mean)
        gz = gmid.astype(BF16)
        gmid_ref[...] = gmid
        gmix_ref[...] = dot_nt(gz, wo[...]).astype(BF16)
        pad = jnp.zeros((gz.shape[0], GRADS - FF - HALF), BF16)
        for h in range(2):

            @pl.when(info[1] == h)
            def _():
                for out, half in ((keep_ref, h), (send_ref, 1 - h)):
                    out[:, FF : FF + HALF] = gz[:, half * HALF : (half + 1) * HALF]
                    out[:, FF + HALF :] = pad


def feed_back(info, grad, grad_rows, wd, wg, wu, up_row, s1, s2, pack, scale, wo):
    rows = 2 * SLOT
    whole = lambda j, info: (0, 0)
    col = pl.BlockSpec((D, FBLOCK), lambda j, info: (0, j))
    wide = pl.BlockSpec((rows, FBLOCK), lambda j, info: (0, j))
    full = pl.BlockSpec((rows, D), whole)
    args = (
        (info,),
        (FF // FBLOCK,),
        (grad, *far(wg, wu, s1, s2), pack, *far(scale, wo)),
        [
            pl.BlockSpec((rows, D), lambda j, info: (info[grad_rows], 0)),
            col,
            pl.BlockSpec((D, FBLOCK), lambda j, info: (up_row, j)),
            wide,
            wide,
            full,
            pl.BlockSpec((rows, LANES), whole),
            pl.BlockSpec((D, D), whole),
        ],
        [
            shape(rows, GRADS),
            shape(rows, GRADS),
            shape(rows, D, dtype=F32),
            shape(rows, D),
        ],
        [
            pl.BlockSpec((rows, GRADS), whole),
            pl.BlockSpec((rows, GRADS), whole),
            full,
            full,
        ],
        cost(2 * rows * D * (3 * FF + D), 24e6),
        [pltpu.VMEM((rows, D), F32)],
    )
    if isinstance(wd, Gathered):
        return launch_loaded(wd, feed_back_kernel, *args)
    prefetch, grid, inputs, in_specs, *rest = args
    in_specs = [*in_specs, pl.BlockSpec((FBLOCK, D), lambda j, info: (j, 0))]
    return launch(feed_back_kernel, prefetch, grid, (*inputs, *far(wd)), in_specs, *rest)


def attention_back_kernel(
    info,
    gmix_ref,
    qkv_ref,
    probs_ref,
    wq,
    wk,
    wv,
    normed_ref,
    scale_ref,
    gmid_ref,
    cos,
    sin_a,
    sin_b,
    gin_ref,
    keep_ref,
    send_ref,
    grads,
):
    for p in range(PAIRS):
        lanes = slice(p * LANES, (p + 1) * LANES)
        gmix = gmix_ref[:, lanes]
        query = head_split(qkv_ref[:, lanes])
        keys = head_split(qkv_ref[:, D + p * LANES : D + (p + 1) * LANES])
        values = head_split(qkv_ref[:, 2 * D + p * LANES : 2 * D + (p + 1) * LANES])
        gmix_parts = head_split(gmix)
        gs_parts = []
        for h in range(2):
            probs = probs_ref[0, 2 * p + h].astype(F32)
            weighted = probs * dot_nt(gmix, values[h])
            inner = jnp.sum(weighted, axis=1, keepdims=True)
            gs_parts.append((weighted - probs * inner).astype(BF16))
        gq = dot(jnp.concatenate(gs_parts, axis=1), jnp.concatenate(keys, axis=0))
        gk = dot_tn(gs_parts[0], query[0]) + dot_tn(gs_parts[1], query[1])
        gv = dot_tn(probs_ref[0, 2 * p], gmix_parts[0]) + dot_tn(
            probs_ref[0, 2 * p + 1], gmix_parts[1]
        )
        gq = gq * cos[...] - turn(gq, sin_a[...], sin_b[...])
        gk = gk * cos[...] - turn(gk, sin_a[...], sin_b[...])
        grads[0, :, lanes] = gq.astype(BF16)
        grads[1, :, lanes] = gk.astype(BF16)
        grads[2, :, lanes] = gv.astype(BF16)
    gn = dot_nt(grads[0], wq[...]) + dot_nt(grads[1], wk[...]) + dot_nt(grads[2], wv[...])
    normed = normed_ref[...].astype(F32)
    mean = jnp.mean(gn * normed, axis=1, keepdims=True)
    gin = gmid_ref[...] + scale_ref[:, :1] * (gn - normed * mean)
    gin_ref[...] = gin.astype(BF16)
    send_ref[:, 3 * HALF :] = gin.astype(BF16)
    for h in range(2):

        @pl.when(info[1] == h)
        def _():
            for out, half in ((keep_ref, h), (send_ref, 1 - h)):
                cols = slice(half * HALF, (half + 1) * HALF)
                for part in range(3):
                    out[:, part * HALF : (part + 1) * HALF] = grads[part, :, cols]


def attention_back(info, gmix, qkv, probs, wq, wk, wv, act, scale, gmid, tables):
    rows = 2 * SLOT
    whole = lambda i, info: (0, 0)
    table = pl.BlockSpec((SLOT, LANES), whole)
    weight = pl.BlockSpec((D, D), whole)
    full = pl.BlockSpec((SLOT, D), lambda i, info: (i, 0))
    pack = pl.BlockSpec((SLOT, 3 * HALF), lambda i, info: (i, 0))
    longer = pl.BlockSpec((SLOT, 5 * HALF), lambda i, info: (i, 0))
    return launch(
        attention_back_kernel,
        (info,),
        (2,),
        (gmix, *far(qkv, probs, wq, wk, wv), act, *far(scale), gmid, *tables),
        [
                full,
                pl.BlockSpec((SLOT, 3 * D), lambda i, info: (i, 0)),
                pl.BlockSpec((1, HEADS, SLOT, SLOT), lambda i, info: (i, 0, 0, 0)),
                weight,
                weight,
                weight,
                full,
                pl.BlockSpec((SLOT, LANES), lambda i, info: (i, 0)),
                full,
                table,
                table,
                table,
            ],
        [shape(rows, D), shape(rows, 3 * HALF), shape(rows, 5 * HALF)],
        [full, pack, longer],
        cost(2 * rows * D * 3 * D + 24 * 8 * 256 * 256 * 128, 16e6),
        [pltpu.VMEM((3, SLOT, D), BF16)],
    )


def spread(info, where, scratch, rows, lane_blocks, outs, row_to):
    for place in range(16):
        if len(outs) == 2:
            low, high = where[0][place], where[1][place]
            shard = info[0] ^ (low + (high - low) * info[1])
        else:
            shard = ((info[0] ^ where[place % 4]) & 12) + place // 4
        at = pl.multiple_of(shard * rows, 16)
        out = outs[place // 8] if len(outs) == 2 else outs[0]
        slot = place % 8 if len(outs) == 2 else place
        for block in range(lane_blocks):
            out[slot, pl.ds(row_to + block * rows, rows), :] = scratch[
                pl.ds(at, rows), block * LANES : (block + 1) * LANES
            ]


def spread_shapes(planar, rows):
    count, dims = (1, (16, rows, LANES)) if planar else (2, (8, rows, LANES))
    return [shape(*dims)] * count, [pl.BlockSpec(dims, lambda j, info: (0, 0, 0))] * count


def feed_weight_kernel(where, gates, downs, info, *refs):
    rows = 2 * SLOT
    steps = FF // FBLOCK
    first = (steps + 1) * gates
    outs = list(refs[: len(refs) - 2 * gates - downs])
    refs = list(refs[len(outs) :])
    if gates:
        (own_ref, oth_ref, act_own, act_oth, g_own, g_oth), outs = outs[:6], outs[6:]
        turned, tile = refs[:2]
    if downs:
        (hid_own, hid_oth, gf_own, gf_oth), outs = outs[:4], outs[4:]
        down = refs[-1]
    step = pl.program_id(0)
    if gates:

        @pl.when(step == 0)
        def _():
            turned[:, :rows] = own_ref[...].T
            turned[:, rows:] = oth_ref[...].T

        @pl.when(step == steps)
        def _():
            turned[:, :rows] = act_own[...].T
            turned[:, rows:] = act_oth[...].T

        @pl.when(step <= steps)
        def _():
            tile[...] = (
                dot(turned[:, :rows], g_own[...]) + dot(turned[:, rows:], g_oth[...])
            ).astype(BF16)

        @pl.when(step < steps)
        def _():
            spread(info, where, tile, 48, 4, outs, pl.multiple_of(step * 192, 16))

        @pl.when(step == steps)
        def _():
            spread(info, where, tile, 48, 3, outs, 768)

    if downs:

        @pl.when(step >= first)
        def _():
            at = pl.multiple_of((step - first) * FBLOCK, FBLOCK)
            down[pl.ds(at, FBLOCK), :] = (
                dot_tn(hid_own[...], gf_own[...]) + dot_tn(hid_oth[...], gf_oth[...])
            ).astype(BF16)

        @pl.when(step == first + steps - 1)
        def _():
            spread(info, where, down, 128, 3, outs, 912 * gates)


def feed_weight(info, where, planar, gates, downs):
    rows = 2 * SLOT
    steps = FF // FBLOCK
    first = (steps + 1) * bool(gates)
    whole = lambda j, info: (0, 0)
    inputs, specs, scratch = [], [], []
    if gates:
        full = pl.BlockSpec((rows, D), whole)
        mixed = pl.BlockSpec((rows, D), lambda j, info: (0, 1))
        grad = pl.BlockSpec((rows, FBLOCK), lambda j, info: (0, jnp.minimum(j, steps)))
        inputs += gates
        specs += [full, full, mixed, mixed, grad, grad]
        scratch += [pltpu.VMEM((D, 2 * rows), BF16), pltpu.VMEM((D, FBLOCK), BF16)]
    if downs:
        *arrays, own_at, oth_at, col = downs
        hid = pl.BlockSpec(
            (rows, FBLOCK), lambda j, info: (0, jnp.maximum(j - first, 0) + PACK // FBLOCK)
        )
        inputs += arrays
        specs += [
            hid,
            hid,
            pl.BlockSpec((rows, HALF), lambda j, info: (info[own_at], info[1])),
            pl.BlockSpec((rows, HALF), lambda j, info: (info[oth_at], col + info[1])),
        ]
        scratch += [pltpu.VMEM((FF, HALF), BF16)]
    out_shape, out_specs = spread_shapes(planar, 912 * bool(gates) + 384 * bool(downs))
    return launch(
        functools.partial(feed_weight_kernel, where, bool(gates), bool(downs)),
        (info,),
        (first + steps * bool(downs),),
        inputs,
        specs,
        out_shape,
        out_specs,
        cost(2 * rows * D * 3 * FF, 20e6),
        scratch,
    )


def attention_weight_kernel(where, info, own_ref, oth_ref, g_own, g_oth, *refs):
    outs, (turned, tile) = refs[:-2], refs[-2:]
    step = pl.program_id(0)
    rows = 2 * SLOT

    @pl.when(step == 0)
    def _():
        turned[:, :rows] = own_ref[...].T
        turned[:, rows:] = oth_ref[...].T

    tile[...] = (
        dot(turned[:, :rows], g_own[...]) + dot(turned[:, rows:], g_oth[...])
    ).astype(BF16)
    spread(info, where, tile, 48, 3, outs, pl.multiple_of(step * 144, 16))


def attention_weight(info, where, planar, own, oth, g_own, g_oth):
    rows = 2 * SLOT
    full = pl.BlockSpec((rows, D), lambda j, info: (0, 0))
    grad = pl.BlockSpec((rows, HALF), lambda j, info: (0, j))
    out_shape, out_specs = spread_shapes(planar, 432)
    return launch(
        functools.partial(attention_weight_kernel, where),
        (info,),
        (3,),
        (own, oth, g_own, g_oth),
        [full, full, grad, grad],
        out_shape,
        out_specs,
        cost(2 * rows * D * 3 * D, 14e6),
        [pltpu.VMEM((D, 2 * rows), BF16), pltpu.VMEM((D, HALF), BF16)],
    )


def gather_plain(section, shards):
    mine = [lax.all_gather(s, "dp", axis=0, tiled=True) for s in shards]
    theirs = [swap(m) for m in mine]
    low = tuple(jnp.where(section == 0, m, t) for m, t in zip(mine, theirs))
    high = tuple(jnp.where(section == 0, t, m) for m, t in zip(mine, theirs))
    return low, high


def unpack_kernel(plan, gained, info, *refs):
    n_src = 1 + max(p[0] for p in plan)
    n_gain = len(gained)
    srcs, refs = refs[: 2 * n_src], refs[2 * n_src :]
    gain, weights, outs = refs[0], refs[1 : 1 + n_gain], refs[1 + n_gain :]
    for section in range(2):

        @pl.when(info[1] == section)
        def _():
            total = jnp.zeros((gain.shape[0], 1), F32)
            for n, (src, row_from, rows, row_to, scale, has_gain, out) in enumerate(plan):
                for side in range(2):
                    piece = srcs[2 * src + (section ^ side)]
                    width = outs[out].shape[1] // 2
                    for block in range(width // LANES):
                        at = row_from + block * rows
                        value = piece[at : at + rows, :]
                        col = side * width + block * LANES
                        if has_gain:
                            weight = weights[gained.index(n)][:, col : col + LANES].astype(F32)
                            total += scale * jnp.sum(weight * value, axis=1, keepdims=True)
                            value = value * (gain[...] * scale)
                        outs[out][row_to : row_to + rows, col : col + LANES] = value
            outs[-1][...] = jnp.broadcast_to(total, outs[-1].shape)


def unpack_all(info, plan, sources, gain, weights, dims):
    gained = tuple(n for n, p in enumerate(plan) if p[5])
    flat = [piece for source in sources for piece in source]
    return launch(
        functools.partial(unpack_kernel, plan, gained),
        (info,),
        (1,),
        (*flat, gain, *weights,),
        [pl.BlockSpec(v.shape, lambda i, info: (0, 0)) for v in (*flat, gain, *weights)],
        [shape(*d, dtype=F32) for d in dims],
        [pl.BlockSpec(d, lambda i, info: (0, 0)) for d in dims],
        cost(0, 8 * sum(a * b for a, b in dims)),
        (),
    )


def on_device(
    tokens,
    heights,
    out_grad,
    w_query,
    w_key,
    w_value,
    w_out,
    w_gate,
    w_up,
    w_down,
    gain_attn,
    gain_ffn,
):
    section = lax.axis_index("section")
    me = lax.axis_index("dp")
    count = lax.axis_size("dp")
    halving = count == 16
    rows = 2 * SLOT
    info = jnp.stack([me, section, 1 - section, jnp.zeros_like(me)]).astype(jnp.int32)
    own_rows, oth_rows, no_rows = 1, 2, 3
    token = [info]
    lim = WIDE * heights + 1
    gain_one = gain_attn[0].astype(F32)[:, None]
    gain_two = gain_ffn[0].astype(F32)[:, None]
    fold = lambda w, g: (w[0].astype(F32) * g).astype(BF16)
    shards = (
        fold(w_query, gain_one * SCALE),
        fold(w_key, gain_one),
        fold(w_value, gain_one),
        w_out[0],
        fold(w_gate, gain_two),
        fold(w_up, gain_two),
        w_down[0],
    )
    half, row = shards[6].shape[0] // 2, shards[0].shape[0]
    tables = tuple(jnp.asarray(t) for t in rope_consts())
    slots = jnp.arange(SLOT)
    valid = (slots[None, :] < lim[:, None]).reshape(-1, 1)
    grad = jnp.where(valid, out_grad, jnp.zeros_like(out_grad))

    def tie(*arrays):
        out = lax.optimization_barrier((*arrays, token[0]))
        token[0] = out[-1]
        return out[:-1] if len(arrays) > 1 else out[0]

    env = {}
    have, parts = {}, {}
    pair = lambda a, b: ((0, row, a, ()), (row, row, b, ()))
    pieces = (
        (pair(0, 1), pair(2, 3)),
        (((0, row, 0, ()),), ((0, row, 1, ()),)),
        (((0, half, 0, (0,)),), ((0, half, 0, (1,)),)),
    )
    if halving:
        dims = (((count, row, D),) * 4, ((count, row, FF),) * 2, ((count, 2, half, D),))
    else:
        dims = (((D, D),) * 4, ((D, FF),) * 2, ((FF, D),))
    flat = lambda found: tuple(w.reshape(-1, w.shape[-1]) for w in found)
    wholes, weights = {}, {}
    if halving:
        groups = (
            (jnp.concatenate(shards[0:2], axis=0), jnp.concatenate(shards[2:4], axis=0)),
            (shards[4], shards[5]),
            (shards[6][:half], shards[6][half:]),
        )
        for n, (first, second) in enumerate(groups):
            mine = jnp.where(section == 0, first, second)
            theirs = swap(jnp.where(section == 0, second, first))
            have[n] = jnp.where(section == 0, mine, theirs)[None]
            have[n + 3] = jnp.where(section == 0, theirs, mine)[None]
    else:
        for layer, found in enumerate(gather_plain(section, shards)):
            for group, some in enumerate((found[:4], found[4:6], found[6:])):
                wholes[3 * layer + group] = Gathered(some, dims[group])

    def double(stream, stage):
        order, after = GATHER[stream]
        if stage:
            env["g", stream, stage - 1] = got = tie(env["g", stream, stage - 1])
            have[stream] = jnp.concatenate([have[stream], got], axis=0)
        elif after is not None:
            env[("g",) + after] = tie(env[("g",) + after])
        have[stream] = tie(have[stream])
        env["g", stream, stage] = flip(
            have[stream], order[stage], count, mirrored(order)[stage]
        )

    def gathered(stream):
        if not halving:
            return wholes[stream]
        if ("q", stream) in env:
            return tie(env["q", stream])
        order = GATHER[stream][0]
        masks = (order_masks(order), order_masks(mirrored(order)))
        theirs, last = tie(env["w", stream], env["v", stream])
        sources = (have[stream], env["g", stream, 3], theirs, last)
        return Gathered(sources, dims[stream % 3], masks, pieces[stream % 3])

    plane = [[4 * z + i for i in range(4)] for z in range(4)]

    def reduce(name):
        env["c", name] = lax.psum_scatter(
            tie(env[name][0]), "dp", scatter_dimension=0, axis_index_groups=plane, tiled=True
        )

    def halve(name, stage):
        order = SCATTER[name]
        if stage:
            parts[name].append(tie(env["r", name, stage - 1]))
        elif len(order) == 2:
            parts[name] = [tie(env["c", name])]
        else:
            parts[name] = [env[name][0]]
        if stage == 0 and len(order) == 4:
            send = env[name][1]
        else:
            size = 1 << (len(order) - stage)
            send = sum(p[size // 2 : size].astype(F32) for p in parts[name]).astype(BF16)
        env["r", name, stage] = flip(tie(send), order[stage], count, mirrored(order)[stage])

    def total(name):
        parts[name].append(tie(env["r", name, len(SCATTER[name]) - 1]))
        env["z", name] = tie(sum(p[0].astype(F32) for p in parts[name]))

    def attend(layer):
        x, x_rows = (tokens, own_rows) if layer == 0 else (env["L", 0], no_rows)
        out = tie(*attention(token[0], lim, x, x_rows, gathered(3 * layer), tables))
        env["A", layer], weights[3 * layer] = out[:4], flat(out[4:])

    def feed_on(layer):
        x, x_rows = (tokens, own_rows) if layer == 0 else (env["L", 0], no_rows)
        w_o, source = weights[3 * layer][3], gathered(3 * layer + 1)
        out = tie(*feed(token[0], x, x_rows, env["A", layer][0], w_o, source))
        env["F", layer] = out[:5]
        weights[3 * layer + 1] = flat(out[5:]) if len(out) > 5 else (source, source)

    def leave_off(layer):
        middle, _, pack, _, _ = env["F", layer]
        w_d = gathered(2) if layer == 0 else weights[5][0]
        out = leave(token[0], lim, middle, pack, w_d)
        out = tie(*out) if len(out) > 1 else (tie(*out),)
        env["L", layer] = out[0]
        if layer == 0:
            weights[2] = flat(out[1:])

    def cotangent(layer):
        if layer == 1:
            return grad, grad, own_rows, oth_rows
        return env["K", 1][0], env.get("xt1"), no_rows, no_rows

    def feed_in(layer):
        own, _, at, _ = cotangent(layer)
        _, scale, pack, s1, s2 = env["F", layer]
        w_g, w_u = weights[3 * layer + 1]
        w_d = gathered(5) if layer == 1 else weights[2][0]
        w_o = weights[3 * layer][3]
        up_row = w_g.shape[0] // D - 1
        out = tie(*feed_back(token[0], own, at, w_d, w_g, w_u, up_row, s1, s2, pack, scale, w_o))
        env["B", layer] = out[:4]
        if layer == 1:
            weights[5] = flat(out[4:])

    def attend_in(layer):
        act, qkv, probs, scale = env["A", layer]
        _, _, gmid, gmix = env["B", layer]
        w = weights[3 * layer][:3]
        env["K", layer] = tie(
            *attention_back(token[0], gmix, qkv, probs, *w, act, scale, gmid, tables)
        )

    def form(name):
        layer = int(name[1])
        order = SCATTER[name][::-1]
        planar = len(order) == 2
        where = order_masks(order) if planar else (order_masks(order), order_masks(mirrored(order)))
        if name[0] in "DG":
            key = "xf%d" % layer
            pack, env[key] = env["F", layer][2], tie(env[key])
            gates, downs = (), ()
            if name[0] == "G":
                more = "xa%d" % layer
                env[more], recv = tie(env[more], env["xs%d" % layer])
                act, keep = env["A", layer][0], env["B", layer][0]
                gates = (pack, env[key], act, env[more], keep, recv)
            if name[0] == "D" or "D%d" % layer not in SCATTER:
                if layer == 0:
                    env["xt1"] = tie(env["xt1"])
                own, oth, at, oth_at = cotangent(layer)
                downs = (pack, env[key], own, oth, at, oth_at, 0 if layer == 1 else 3)
            made = feed_weight(token[0], where, planar, gates, downs)
        else:
            more = "xa%d" % layer
            env[more], recv = tie(env[more], env["xt%d" % layer])
            other = env[more]
            args = (env["A", layer][0], other, env["K", layer][1], recv)
            made = attention_weight(token[0], where, planar, *args)
        env[name] = tie(*made) if len(made) > 1 else (tie(*made),)

    sent = {
        "a": lambda layer: env["A", layer][0],
        "f": lambda layer: env["F", layer][2],
        "s": lambda layer: env["B", layer][1],
        "t": lambda layer: env["K", layer][2],
    }

    def both(mine, theirs):
        low = jnp.concatenate([mine, theirs], axis=0)
        return jnp.where(section == 0, low, jnp.concatenate([theirs, mine], axis=0))[None]

    pick = lambda first, second: jnp.where(section == 0, first, second)

    def unpacked(names, plan, gain, local, out_dims):
        sources = [(env["m", n], tie(env["h", n])) for n in names]
        return unpack_all(token[0], plan, sources, gain, local, out_dims)

    def run(name):
        kind, rest = name[0], name[1:]
        if kind == "g":
            double(int(rest[0]), int(rest[1]))
        elif kind == "w":
            env["w", int(rest)] = swap(tie(have[int(rest)]))
        elif kind == "v":
            key = ("g", int(rest), 3)
            env[key] = tie(env[key])
            env["v", int(rest)] = swap(env[key])
        elif kind == "q":
            stream = int(rest)
            part = tie(have[stream])[0]
            env["q", stream] = lax.all_gather(part, ("section", "dp"), tiled=True)
        elif kind == "c":
            reduce(rest)
        elif kind == "r":
            halve(rest[:2], int(rest[2]))
        elif kind == "z":
            total(rest)
        elif kind == "d":
            kind, rest = rest[0], rest[1:]
            keys = {
                "g": lambda: ("g", int(rest[0]), int(rest[1])),
                "r": lambda: ("r", rest[:2], int(rest[2])),
                "x": lambda: "x" + rest,
                "o": lambda: "o" + rest,
                "h": lambda: ("h", rest),
                "c": lambda: ("c", rest),
            }
            key = keys.get(kind, lambda: (kind, int(rest)))()
            env[key] = tie(env[key])
        elif kind == "x":
            env[name] = swap(tie(sent[rest[0]](int(rest[1]))))
        elif kind == "h":
            first, second = (
                jnp.concatenate([env["z", k + at] for k in rest + "D" if ("z", k + at) in env])
                if rest == "G"
                else env["z", rest + at]
                for at in "01"
            )
            env["m", rest], other = tie(pick(first, second), pick(second, first))
            env["h", rest] = swap(other)
        elif name == "u1":
            side = row * FHALF // LANES
            last = 2 * side + row * HALF // LANES
            plan = (
                (0, 0, row, 0, 1.0, True, 0),
                (0, side, row, 0, 1.0, True, 1),
                (0, 2 * side, row, 0, 1.0, False, 2),
                (0, last, 2 * half, 0, 1.0, False, 3),
            )
            out_dims = ((row, FF), (row, FF), (row, D), (2 * half, D), (row, LANES))
            env["u1"] = unpacked("G", plan, gain_two, (w_gate[0], w_up[0]), out_dims)
        elif name == "u2":
            side = row * HALF // LANES
            plan = (
                (0, 0, row, 0, SCALE, True, 0),
                (0, side, row, 0, 1.0, True, 1),
                (0, 2 * side, row, 0, 1.0, True, 2),
            )
            local = (w_query[0], w_key[0], w_value[0])
            out_dims = ((row, D),) * 3 + ((row, LANES),)
            env["u2"] = unpacked("T", plan, gain_one, local, out_dims)
        elif name == "oa":
            env["oa"] = swap(tie(pick(env["L", 1], env["L", 0])))
        elif name == "ob":
            env["ob"] = both(pick(env["L", 0], env["L", 1]), tie(env["oa"]))
        elif name == "oi":
            other = [v[:, 3 * HALF :] for v in tie(env["xt0"], env["xt1"])]
            env["oi"] = both(pick(env["K", 0][0], env["K", 1][0]), pick(*other))
        else:
            layer = int(rest)
            {"A": attend, "F": feed_on, "L": leave_off, "B": feed_in, "K": attend_in}[kind](layer)

    for name in ORDER:
        if name[0] in "DGT":
            if halving:
                form(name)
        elif halving or name[0] in "xoAFLBK":
            run(name)

    if halving:
        grad_g, grad_u, grad_o, grad_d, gain_grad_two = env["u1"]
        grad_q, grad_k, grad_v, gain_grad_one = env["u2"]
        gain_grad_one, gain_grad_two = gain_grad_one[:, 0], gain_grad_two[:, 0]
    else:
        cut = lambda v, at: lax.dynamic_slice_in_dim(v, info[at] * rows, rows, 0)
        join = lambda a, b: jnp.concatenate([a, b], axis=0)

        def reduced(a, g):
            full = lax.dot_general(a, g, (((0,), (0,)), ((), ())), preferred_element_type=F32)
            return lax.psum_scatter(full, "dp", scatter_dimension=0, tiled=True)

        found = []
        for layer in range(2):
            own, oth, at, oth_at = cotangent(layer)
            oth = oth if layer == 1 else oth[:, 3 * HALF :]
            gf = lax.dynamic_slice_in_dim(
                join(cut(own, at), cut(oth, oth_at)), section * HALF, HALF, 1
            )
            acts = join(env["A", layer][0], env["xa%d" % layer])
            gts = join(env["K", layer][1], env["xt%d" % layer][:, : 3 * HALF])
            gus = join(env["B", layer][0], env["xs%d" % layer])
            pack = join(env["F", layer][2], env["xf%d" % layer])
            nor, hid = pack[:, :D], pack[:, PACK:]
            found.append(
                (
                    reduced(acts[:, :D], gts[:, :HALF]),
                    reduced(acts[:, :D], gts[:, HALF : 2 * HALF]),
                    reduced(acts[:, :D], gts[:, 2 * HALF :]),
                    reduced(acts[:, D:], gus[:, FF : FF + HALF]),
                    reduced(nor, gus[:, :FHALF]),
                    reduced(nor, gus[:, FHALF:FF]),
                    reduced(hid, gf),
                )
            )

        def cols(first, second):
            mine, theirs = pick(first, second), swap(pick(second, first))
            low = jnp.concatenate([mine, theirs], axis=1)
            return pick(low, jnp.concatenate([theirs, mine], axis=1))

        grads = [cols(first, second) for first, second in zip(*found)]
        grad_q, grad_k, grad_v, grad_o, grad_g, grad_u, grad_d = grads
        along = lambda w, g: jnp.sum(w[0].astype(F32) * g, axis=1)
        gain_grad_one = SCALE * along(w_query, grad_q)
        gain_grad_one += along(w_key, grad_k) + along(w_value, grad_v)
        gain_grad_two = along(w_gate, grad_g) + along(w_up, grad_u)
        grad_q, grad_k, grad_v = grad_q * (gain_one * SCALE), grad_k * gain_one, grad_v * gain_one
        grad_g, grad_u = grad_g * gain_two, grad_u * gain_two

    return (
        env["ob"],
        env["oi"],
        grad_q[None],
        grad_k[None],
        grad_v[None],
        grad_o[None],
        grad_g[None],
        grad_u[None],
        grad_d[None],
        gain_grad_one[None],
        gain_grad_two[None],
    )


def solution(mesh):
    rows = P("dp", None)
    weight = P("section", "dp", None)
    gain = P("section", "dp")
    return jax.shard_map(
        on_device,
        mesh=mesh,
        in_specs=(rows, P("dp"), rows) + (weight,) * 7 + (gain,) * 2,
        out_specs=(weight,) * 9 + (gain,) * 2,
        check_vma=False,
    )
```
